32 devices in a mesh: dp: 8 (over z, y), mp: 4 (over x, core).
Axes of the slice: x: 2, y: 2, z: 4, core: 2. Of those that a mesh axis runs over, the one named last changes fastest.
Arguments:
- patches: bfloat16 [15360, 128], P(('dp', 'mp')), may hold values from -6 to 6
- row_count: int32 [32], P(('dp', 'mp')), may hold values from 0 to 480, as said below
- target_group: int32 [15360], P(('dp', 'mp')), may hold values from 0 to 7, as said below
- target_offset: int32 [15360], P(('dp', 'mp')), may hold values from 0 to 639, as said below
- embed: bfloat16 [128, 6144], replicated, may hold values from -0.5 to 0.5
- norm_gain: bfloat16 [6144], replicated, may hold values from 0.099609375 to 1.8984375
- readout: bfloat16 [6144, 128], P('mp'), may hold values from -0.078125 to 0.078125
- target: bfloat16 [5120, 128], P('dp'), may hold values from -12 to 12
- master: float32 [6144, 6144], P('dp', 'mp'), may hold values from -6 to 6
- moment1: float32 [6144, 6144], P('dp', 'mp'), may hold values from -2 to 2
- moment2: float32 [6144, 6144], P('dp', 'mp'), may hold values from 0.00086805556 to 0.034722224
Outputs:
- prediction: float32 [5120, 128], P('dp')
- master_new: float32 [6144, 6144], P('dp', 'mp')
- moment1_new: float32 [6144, 6144], P('dp', 'mp')
- moment2_new: float32 [6144, 6144], P('dp', 'mp')
- weight_copy: bfloat16 [6144, 6144], P('dp', 'mp')
The draws below stay inside these ranges and needn't reach their ends.
Inputs may be any that keep to these rules, and one draw needn't show every extreme that they name: Device i holds its live patch rows in its first row_count[i] slots; some device holds 480 of them in every draw. Over the live slots of all devices, each pair (target_group, target_offset) of the 5120 positions occurs exactly once; values in slots past row_count are arbitrary within the range. Call target_offset // 160 the block of a row. Each (batch, block) receives exactly 160 live rows; one device sends at most 15 live rows to one (batch, block), and every (batch, block) gets 15 rows from some device.
All inputs are finite; a program needn't handle non-finite values.
Results may differ from the reference program's by a relative error of at most 0.03.
Values may be sent and summed in bfloat16 or wider, within the bound.
No kernel may reach another device: no remote copies, remote signals or barrier semaphores. Data moves between devices by JAX's collectives and lax.ppermute only.
A program may use at most 128 MiB of HBM per device.

```python
import math
import jax
import jax.numpy as jnp
from jax import lax

D = 6144
PATCH = 128
TOK_DEV = 640
TOKENS = 5120
QUART = 160
CAP = 15
SLOTS = 480
N_DP = 8
N_MP = 4
DEVICES = 32


def route_plan(key):
    base_key = jax.random.fold_in(key, 7)
    keys = jax.random.split(base_key, 7)
    devices_all = N_DP * N_MP
    order_draw = jax.random.permutation(keys[0], devices_all)
    heavy_flag = (order_draw < 4).astype(jnp.int32)
    bias_draw = jax.random.randint(keys[1], (devices_all,), 0, 4)
    noise_draw = jax.random.randint(keys[2], (devices_all, devices_all), 0, 65536)
    scores = (heavy_flag * 8 + bias_draw)[None, :] * 65536 + noise_draw
    scores = scores * devices_all + jnp.arange(devices_all, dtype=jnp.int32)[None, :]
    ranking = jnp.argsort(jnp.argsort(-scores, axis=1), axis=1).astype(jnp.int32)
    sent = jnp.clip(QUART - ranking * CAP, 0, CAP).T
    source_rank = ranking.T
    load = jnp.sum(sent, axis=1).astype(jnp.int32)
    cumulative = jnp.cumsum(sent, axis=1)
    starting = cumulative - sent
    slot_ids = jnp.arange(SLOTS, dtype=jnp.int32)
    dest_index = jnp.sum((cumulative[:, None, :] <= slot_ids[None, :, None]).astype(jnp.int32), axis=2)
    dest_clip = jnp.minimum(dest_index, devices_all - 1)
    within = slot_ids[None, :] - jnp.take_along_axis(starting, dest_clip, axis=1)
    rank_here = jnp.take_along_axis(source_rank, dest_clip, axis=1)
    column_perms = jax.vmap(lambda sub_key: jax.random.permutation(sub_key, QUART))(jax.random.split(keys[3], devices_all)).astype(jnp.int32)
    position = jnp.clip(rank_here * CAP + within, 0, QUART - 1)
    local_place = column_perms[dest_clip, position]
    occupied = slot_ids[None, :] < load[:, None]
    group_live = dest_clip // N_MP
    offset_live = dest_clip % N_MP * QUART + local_place
    group_junk = jax.random.randint(keys[4], (devices_all, SLOTS), 0, N_DP)
    offset_junk = jax.random.randint(keys[5], (devices_all, SLOTS), 0, TOK_DEV)
    group_all = jnp.where(occupied, group_live, group_junk).astype(jnp.int32)
    offset_all = jnp.where(occupied, offset_live, offset_junk).astype(jnp.int32)
    shuffle_key = (1 - occupied.astype(jnp.int32)) * 65536 + jax.random.randint(keys[6], (devices_all, SLOTS), 0, 65536)
    shuffle_key = shuffle_key * SLOTS + slot_ids[None, :]
    reorder = jnp.argsort(shuffle_key, axis=1)
    group_all = jnp.take_along_axis(group_all, reorder, axis=1)
    offset_all = jnp.take_along_axis(offset_all, reorder, axis=1)
    return (load, group_all.reshape(-1), offset_all.reshape(-1))


def draw_row_count(key, part):
    return route_plan(key)[0]


def draw_target_group(key, part):
    return route_plan(key)[1]


def draw_target_offset(key, part):
    return route_plan(key)[2]


def shard_levels(stream_key, extent, pieces, low, largest):
    loudness, own = 1.0, jax.random.fold_in(stream_key, 6)
    for dim, shards_of in pieces:
        heights = jnp.exp(jax.random.uniform(jax.random.fold_in(own, dim), (shards_of,), jnp.float32, low / len(pieces), largest / len(pieces)))
        loudness = loudness * jnp.repeat(heights, extent[dim] // shards_of).reshape([-1 if axis == dim else 1 for axis in range(len(extent))])
    return loudness


def centred(stream_key, extent, spread, reach, shards=(), kind=jnp.bfloat16):
    drawn = spread * jax.random.normal(stream_key, extent, jnp.float32)
    if shards:
        drawn = drawn * shard_levels(stream_key, extent, shards, -0.22, 0.18)
    return jnp.clip(drawn, -reach, reach).astype(kind)


def setup_inputs(seed: int = 0) -> dict:
    streams_of = jax.random.split(jax.random.key(seed), 12)
    return {
        "patches": centred(streams_of[0], (DEVICES * SLOTS, PATCH), 1.0, 6.0, ((0, 32),)),
        "row_count": draw_row_count(jax.random.fold_in(streams_of[11], 71), 0),
        "target_group": draw_target_group(jax.random.fold_in(streams_of[11], 71), 0),
        "target_offset": draw_target_offset(jax.random.fold_in(streams_of[11], 71), 0),
        "embed": centred(streams_of[4], (PATCH, D), PATCH ** -0.5, 0.5),
        "norm_gain": jnp.clip(1.0 + 0.18 * jax.random.normal(streams_of[5], (D,), jnp.float32), 0.099609375, 1.8984375).astype(jnp.bfloat16),
        "readout": centred(streams_of[6], (D, PATCH), D ** -0.5, 0.078125, ((0, 4),)),
        "target": centred(streams_of[7], (TOKENS, PATCH), 3.0, 12.0, ((0, 8),)),
        "master": centred(streams_of[8], (D, D), 1.0, 6.0, ((0, 8), (1, 4)), jnp.float32),
        "moment1": centred(streams_of[9], (D, D), 0.3, 2.0, ((0, 8), (1, 4)), jnp.float32),
        "moment2": jnp.clip(jnp.exp(math.log(0.034722224) - 3.6888795 * jax.random.uniform(streams_of[10], (D, D), jnp.float32) ** shard_levels(streams_of[10], (D, D), ((0, 8), (1, 4)), -0.2, 0.2)), 0.00086805556, 0.034722224),
    }


gelu_const = 0.7978845608028654
beta_one = 0.9
beta_two = 0.95
learn_rate = 0.01
decay_rate = 0.1
adam_epsilon = 1e-08
step_count = 20

def gelu_tanh(value):
    inner = gelu_const * (value + 0.044715 * value * value * value)
    return 0.5 * value * (1.0 + jnp.tanh(inner))

def gelu_slope(value):
    tangent = jnp.tanh(gelu_const * (value + 0.044715 * value * value * value))
    return 0.5 * (1.0 + tangent) + 0.5 * value * (1.0 - tangent * tangent) * gelu_const * (1.0 + 3.0 * 0.044715 * value * value)

def reference(patches, row_count, target_group, target_offset, embed, norm_gain, readout, target, master, moment1, moment2):
    occupied = (jnp.arange(SLOTS, dtype=jnp.int32)[None, :] < row_count[:, None]).reshape(-1)
    placed = jnp.where(occupied, target_group * TOK_DEV + target_offset, TOKENS).astype(jnp.int32)
    batch = jnp.zeros((TOKENS, PATCH), jnp.bfloat16).at[placed].set(patches, mode='drop')
    weight = master.astype(jnp.bfloat16)
    width_scale = 1.0 / D ** 0.5
    gain_wide = norm_gain.astype(jnp.float32)

    def group_step(gradient, inputs):
        patch_block, goal = inputs
        hidden = gelu_tanh(jnp.dot(patch_block, embed, preferred_element_type=jnp.float32))
        normed = (hidden * lax.rsqrt(lax.optimization_barrier(jnp.mean(hidden * hidden, axis=-1, keepdims=True)) + 1e-05) * gain_wide).astype(jnp.bfloat16)
        preact = jnp.dot(normed, weight, preferred_element_type=jnp.float32) * width_scale
        activation = gelu_tanh(preact).astype(jnp.bfloat16)
        prediction = jnp.dot(activation, readout, preferred_element_type=jnp.float32)
        errors = (prediction - goal.astype(jnp.float32)).astype(jnp.bfloat16)
        backward = jnp.dot(errors, readout.T, preferred_element_type=jnp.float32)
        delta_rows = (backward * gelu_slope(preact)).astype(jnp.bfloat16)
        term = (jnp.dot(normed.T, delta_rows, preferred_element_type=jnp.float32) * width_scale).astype(jnp.bfloat16)
        term = lax.optimization_barrier(term).astype(jnp.float32)
        return (gradient + term, prediction)
    gradient, predicted = lax.scan(group_step, jnp.zeros((D, D), jnp.float32), (batch.reshape(N_DP, TOK_DEV, PATCH), target.reshape(N_DP, TOK_DEV, PATCH)))
    moment1_new = beta_one * moment1 + (1.0 - beta_one) * gradient
    moment2_new = beta_two * moment2 + (1.0 - beta_two) * gradient * gradient
    first_fix = moment1_new / (1.0 - beta_one ** step_count)
    second_fix = moment2_new / (1.0 - beta_two ** step_count)
    master_new = master - learn_rate * (first_fix / (jnp.sqrt(second_fix) + adam_epsilon) + decay_rate * master)
    return (predicted.reshape(TOKENS, PATCH), master_new, moment1_new, moment2_new, master_new.astype(jnp.bfloat16))
```

```python
import jax
import jax.numpy as jnp
from jax import lax
from jax.experimental import pallas as pl
from jax.experimental.pallas import tpu as pltpu
from jax.sharding import PartitionSpec as P

gelu_const = 0.7978845608028654
beta_one = 0.9
beta_two = 0.95
learn_rate = 0.01
decay_rate = 0.1
adam_epsilon = 1e-08
step_count = 20

line = 4
groups = 2
pieces = 4
streams = 2


def gelu_tanh(value):
    inner = value * (gelu_const + (gelu_const * 0.044715) * (value * value))
    half = 0.5 * value
    return half + half * jnp.tanh(inner)


def gelu_slope(value):
    square = value * value
    tangent = jnp.tanh(value * (gelu_const + (gelu_const * 0.044715) * square))
    return 0.5 * (1.0 + tangent) + value * (1.0 - tangent * tangent) * (
        0.5 * gelu_const + (1.5 * gelu_const * 0.044715) * square
    )


def dot32(left, right):
    return jnp.dot(left, right, preferred_element_type=jnp.float32)


def route(patches, row_count, target_group, target_offset, block_rows):
    model_count, batch_count = lax.axis_size("mp"), lax.axis_size("dp")
    inner = batch_count // line
    devices_all = batch_count * model_count
    columns_all = inner * model_count
    slot_total, patch_width = patches.shape
    capacity = slot_total // devices_all
    lot = capacity + 1
    occupied = jnp.arange(slot_total, dtype=jnp.int32) < row_count[0]
    column = target_group % inner * model_count + target_offset // block_rows
    owner = jnp.where(occupied, column * line + target_group // inner, devices_all)
    onehot = (owner[:, None] == jnp.arange(devices_all, dtype=jnp.int32)[None, :]).astype(
        jnp.int32
    )
    placing = jnp.sum(onehot * jnp.cumsum(onehot, axis=0), axis=1) - 1
    slot = jnp.where(occupied, owner * lot + placing, devices_all * lot)
    spread = (jnp.arange(devices_all * lot, dtype=jnp.int32)[:, None] == slot[None, :]).astype(
        jnp.bfloat16
    )
    rows = dot32(spread, patches).astype(jnp.bfloat16).reshape(devices_all, lot, patch_width)
    lanes = (placing[:, None] == jnp.arange(patch_width, dtype=jnp.int32)[None, :]).astype(
        jnp.bfloat16
    )
    shifted = onehot * (target_offset % block_rows - block_rows)[:, None]
    marks = block_rows + lax.dot_general(
        shifted.astype(jnp.bfloat16),
        lanes,
        (((0,), (0,)), ((), ())),
        preferred_element_type=jnp.float32,
    )
    last = lax.broadcasted_iota(jnp.int32, rows.shape, 1) == capacity
    outgoing = jnp.where(last, marks.astype(jnp.bfloat16)[:, None, :], rows)
    outgoing = outgoing.reshape(1, columns_all, line * lot, patch_width)
    outgoing = jnp.broadcast_to(outgoing, (line,) + outgoing.shape[1:])
    arrived = lax.all_to_all(
        outgoing.reshape(devices_all, line * lot, patch_width),
        ("dp", "mp"),
        split_axis=0,
        concat_axis=0,
        tiled=True,
    )
    places = arrived.reshape(devices_all, line, lot, patch_width)[:, :, capacity, :lot]
    places = places.astype(jnp.int32)
    offsets = jnp.arange(line, dtype=jnp.int32)[None, :, None] * block_rows
    places = jnp.where(places < block_rows, places + offsets, line * block_rows)
    gather = (
        places.reshape(1, devices_all * line * lot)
        == jnp.arange(line * block_rows, dtype=jnp.int32)[:, None]
    ).astype(jnp.bfloat16)
    return dot32(gather, arrived.reshape(devices_all * line * lot, patch_width)).astype(
        jnp.bfloat16
    )


def adam_kernel(own_ref, came_ref, master_ref, moment1_ref, moment2_ref, *refs):
    master_out, moment1_out, moment2_out, copy_out = refs[-4:]
    gradient = own_ref[...] + came_ref[...].astype(jnp.float32)
    moment1_new = beta_one * moment1_ref[...] + (1.0 - beta_one) * gradient
    moment2_new = beta_two * moment2_ref[...] + (1.0 - beta_two) * gradient * gradient
    first_fix = moment1_new / (1.0 - beta_one**step_count)
    second_fix = moment2_new / (1.0 - beta_two**step_count)
    master = master_ref[...]
    master_new = master - learn_rate * (
        first_fix / (jnp.sqrt(second_fix) + adam_epsilon) + decay_rate * master
    )
    master_out[...] = master_new
    moment1_out[...] = moment1_new
    moment2_out[...] = moment2_new
    copy_out[...] = master_new.astype(jnp.bfloat16)


def adam_piece(own, came, state, outs, which):
    depth, cut = own.shape
    tile = depth // 3
    piece = pl.BlockSpec((tile, cut), lambda i: (i, 0))
    column = pl.BlockSpec((tile, cut), lambda i: (i, which))
    whole = [jax.ShapeDtypeStruct(state[0].shape, jnp.float32)] * 3
    whole.append(jax.ShapeDtypeStruct(state[0].shape, jnp.bfloat16))
    outs = outs or []
    return pl.pallas_call(
        adam_kernel,
        grid=(3,),
        in_specs=[piece, piece, column, column, column]
        + [pl.BlockSpec(memory_space=pl.ANY)] * len(outs),
        out_specs=[column] * 4,
        out_shape=whole,
        input_output_aliases={5 + i: i for i in range(len(outs))},
        compiler_params=pltpu.CompilerParams(vmem_limit_bytes=24 * 1024 * 1024),
        cost_estimate=pl.CostEstimate(
            flops=20 * depth * cut, bytes_accessed=32 * depth * cut, transcendentals=depth * cut
        ),
        name="adam_piece",
    )(own, came, *state, *outs)


def shards(
    patches,
    row_count,
    target_group,
    target_offset,
    embed,
    norm_gain,
    readout,
    target,
    master,
    moment1,
    moment2,
):
    model_count, batch_count = lax.axis_size("mp"), lax.axis_size("dp")
    inner = batch_count // line
    place = lax.axis_index("dp") // inner
    inside = lax.axis_index("dp") % inner
    last = line - 1
    at_end = (place == 0) | (place == last)
    far_side = place >= line // 2
    batch_rows = target.shape[0]
    block_rows = batch_rows // model_count
    width = embed.shape[1]
    patch_width = embed.shape[0]
    depth, columns = master.shape
    width_scale = 1.0 / width**0.5

    def swap(value, partners):
        pairs = [
            (p * inner + q, r * inner + q)
            for one, two in partners
            for p, r in ((one, two), (two, one))
            for q in range(inner)
        ]
        return lax.ppermute(value, "dp", pairs)

    def swap_end(value):
        return swap(value, ((0, 1), (last - 1, last)))

    def swap_middle(value):
        return swap(value, ((1, 2),))

    def turn(value, step):
        pairs = [
            (p * inner + q, p * inner + (q + step) % inner)
            for p in range(line)
            for q in range(inner)
        ]
        return lax.ppermute(value, "dp", pairs)

    def mp_sum(value, kind):
        step = 1
        while step < model_count:
            value = value.astype(kind)
            other = lax.ppermute(value, "mp", [(m, m ^ step) for m in range(model_count)])
            value = value.astype(jnp.float32) + other.astype(jnp.float32)
            step *= 2
        return value

    cut = columns // pieces
    lot = pieces // 2
    slices = [slice(piece * cut, (piece + 1) * cut) for piece in range(pieces)]
    weight_own = [
        master[:, first * cut : (first + lot) * cut].astype(jnp.bfloat16)
        for first in range(0, pieces, lot)
    ]
    weight_own[0], patches, target_offset = lax.optimization_barrier(
        (weight_own[0], patches, target_offset)
    )
    weight = []

    def gather_weight():
        rows = weight_own[len(weight)]
        if weight:
            rows, weight[-1] = lax.optimization_barrier((rows, weight[-1]))
        weight.append([rows] + [turn(rows, -step) for step in range(1, inner)])

    def weight_piece(piece):
        cols = slices[piece % lot]
        return jnp.concatenate([rows[:, cols] for rows in weight[piece // lot]], axis=0)

    gather_weight()
    target_other = swap_end(target)

    blocks = route(patches, row_count, target_group, target_offset, block_rows)
    batches = lax.all_gather(blocks.reshape(line, block_rows, -1), "mp", axis=1, tiled=True)
    outbound = [jnp.where(far_side, batches[g], batches[last - g]) for g in range(groups)]
    inbound = [jnp.where(far_side, batches[last - g], batches[g]) for g in range(groups)]

    starts = [(place * inner + (inside + step) % inner) * depth for step in range(inner)]
    embed_here = jnp.concatenate(
        [lax.dynamic_slice_in_dim(embed, start, depth, axis=1) for start in starts], axis=1
    )
    gain_here = jnp.concatenate(
        [lax.dynamic_slice_in_dim(norm_gain, start, depth, axis=0) for start in starts], axis=0
    ).astype(jnp.float32)

    def make_features(tokens):
        return (gelu_tanh(dot32(tokens, embed_here)) * gain_here).astype(jnp.bfloat16)

    def local_scales():
        share = lax.axis_index("mp") * block_rows
        mine = jnp.concatenate(
            [lax.dynamic_slice_in_dim(tokens, share, block_rows, axis=0) for tokens in inbound],
            axis=0,
        )
        hidden = gelu_tanh(dot32(mine, embed))
        return lax.rsqrt(jnp.mean(hidden * hidden, axis=-1) + 1e-05) * width_scale

    def all_scales(scale):
        placed = jnp.zeros((groups, model_count, block_rows), jnp.float32)
        placed = lax.dynamic_update_slice_in_dim(
            placed, scale.reshape(groups, 1, block_rows), lax.axis_index("mp"), axis=1
        )
        placed = mp_sum(placed.reshape(groups, batch_rows), jnp.float32)
        return [placed[g][:, None] for g in range(groups)]

    units = groups * pieces
    goals = [target, target_other]
    rows_each = batch_rows // streams
    parts = [slice(part * rows_each, (part + 1) * rows_each) for part in range(streams)]
    features, scales, predicted, errors = [], [], [], []
    sums, preact, partial, delta = {}, {}, {}, {}
    ends, middles = {}, {}
    whole_parts = {}
    early, pending, outs = {}, {}, None

    def wide(value):
        return value.astype(jnp.float32)

    def group_features(group):
        return make_features(jnp.concatenate([outbound[group], inbound[group]], axis=0))

    def partial_sums(unit):
        group, piece = divmod(unit, pieces)
        right = weight_piece(piece)
        return [
            dot32(features[group][side * batch_rows :][:batch_rows], right).astype(jnp.bfloat16)
            for side in range(2)
        ]

    def finished(part, unit, before):
        group, piece = divmod(unit, pieces)
        value = (wide(sums[unit][1][parts[part]]) + wide(before)) * scales[group][parts[part]]
        active = gelu_tanh(value).astype(jnp.bfloat16)
        return value, dot32(active, readout[slices[piece]])

    def new_delta(part, unit, before):
        group, piece = divmod(unit, pieces)
        back = lax.dot_general(
            lax.optimization_barrier((errors[group][parts[part]], before))[0],
            readout[slices[piece]],
            (((1,), (1,)), ((), ())),
            preferred_element_type=jnp.float32,
        )
        slope = gelu_slope(preact[part, unit])
        return (back * slope * scales[group][parts[part]]).astype(jnp.bfloat16)

    def gradient_term(unit, rows):
        first = units + unit
        arrived = [
            jnp.where(at_end, ends[part, first + 2], middles[part, first + 1])
            for part in range(streams)
        ] + [jnp.where(at_end, delta[part, unit], ends[part, first]) for part in range(streams)]
        return lax.dot_general(
            features[unit // pieces][:, rows],
            jnp.concatenate(arrived, axis=0),
            (((0,), (0,)), ((), ())),
            preferred_element_type=jnp.float32,
        )

    features.append(group_features(0))
    sums[0] = partial_sums(0)
    gather_weight()
    side_work = {
        (0, 0): [1, "scales"],
        (0, streams - 1): ["features"],
        (1, 0): [4, 5],
        (1, streams - 1): [2],
        (2, 0): [3],
        (2, streams - 1): [6, 7],
    }
    for tick, part in [(t, p) for t in range(2 * units + line) for p in range(streams)]:
        back_tick = tick - units
        was_end = was_middle = None
        if tick:
            was_end, was_middle, pending = lax.optimization_barrier(
                (ends.get((part, tick - 1)), middles.get((part, tick - 1)), pending)
            )
            ends[part, tick - 1], middles[part, tick - 1] = was_end, was_middle
            for box, key in list(pending):
                value = pending.pop((box, key))
                if box == "sums":
                    sums[key] = value
                elif box == "preact":
                    preact[key], partial[key] = value
                elif box == "delta":
                    delta[key] = value
                elif box == "early":
                    early[key] = value
                elif box == "features":
                    features.append(value)
                else:
                    scales = all_scales(value)

        from_end = from_middle = None
        if tick < units:
            from_end = sums[tick][0][parts[part]]
        elif back_tick < units:
            from_end = delta[part, back_tick]
        elif back_tick == units:
            narrow = predicted[1][parts[part]].astype(jnp.bfloat16)
            from_end = jnp.pad(narrow, ((0, 0), (0, cut - patch_width)))
        if 2 <= tick < units + 2:
            from_middle = (wide(sums[tick - 2][1][parts[part]]) + wide(was_middle)).astype(jnp.bfloat16)
        elif 2 <= back_tick < units + 2:
            from_middle = was_middle
        if from_end is None or from_middle is None:
            payload = from_middle if from_end is None else from_end
        else:
            payload = jnp.where(at_end, from_end, from_middle)
        if payload is not None:
            ends[part, tick] = swap_end(payload)
        if 1 <= tick < units + 1:
            payload = (wide(sums[tick - 1][0][parts[part]]) + wide(was_end)).astype(jnp.bfloat16)
            middles[part, tick] = swap_middle(payload)
        elif 1 <= back_tick < units + 1:
            middles[part, tick] = swap_middle(was_end)

        for work in side_work.get((tick, part), ()):
            if work == "scales":
                pending["scales", None] = local_scales()
            elif work == "features":
                pending["features", None] = group_features(1)
            else:
                pending["sums", work] = partial_sums(work)

        unit = tick - line + 1
        if 0 <= unit < units:
            group, piece = divmod(unit, pieces)
            value = finished(part, unit, was_end)
            pending["preact", (part, unit)] = value
            if piece == pieces - 1:
                whole = sum(partial[part, unit - back] for back in range(1, pieces)) + value[1]
                whole_parts[part] = whole
                if part == streams - 1:
                    whole = [whole_parts[other] for other in range(streams)]
                    predicted.append(mp_sum(jnp.concatenate(whole, axis=0), jnp.bfloat16))
                    errors.append((predicted[-1] - wide(goals[group])).astype(jnp.bfloat16))

        unit = back_tick + 1
        if 0 <= unit < units:
            pending["delta", (part, unit)] = new_delta(part, unit, was_end)

        unit = back_tick - line + 1
        if 0 <= unit < units and part == streams - 1:
            group, piece = divmod(unit, pieces)
            if group < groups - 1:
                pending["early", (group, piece)] = gradient_term(unit, slice(None))
            else:
                total = None
                for step in [*range(1, inner), 0]:
                    rows = slice(step * depth, (step + 1) * depth)
                    value = gradient_term(unit, rows)
                    for other in range(groups - 1):
                        value += early[other, piece][rows]
                    if step == 0:
                        outs = adam_piece(value, total, (master, moment1, moment2), outs, piece)
                    else:
                        value = turn(value.astype(jnp.bfloat16), step)
                        total = value if total is None else (wide(total) + wide(value)).astype(
                            jnp.bfloat16
                        )

    from_ends = [ends[part, 2 * units][:, :patch_width] for part in range(streams)]
    prediction = jnp.where(at_end, predicted[0], wide(jnp.concatenate(from_ends, axis=0)))
    return (prediction, *outs)


def solution(mesh):
    placed = (
        P(("dp", "mp"), None),
        P(("dp", "mp")),
        P(("dp", "mp")),
        P(("dp", "mp")),
        P(),
        P(),
        P("mp", None),
        P("dp", None),
        P("dp", "mp"),
        P("dp", "mp"),
        P("dp", "mp"),
    )
    return jax.shard_map(
        shards,
        mesh=mesh,
        in_specs=placed,
        out_specs=(P("dp", None), P("dp", "mp"), P("dp", "mp"), P("dp", "mp"), P("dp", "mp")),
        check_vma=False,
    )
```

```python
import jax
import jax.numpy as jnp
from jax import lax
from jax.experimental import pallas as pl
from jax.experimental.pallas import tpu as pltpu
from jax.sharding import PartitionSpec as P

gelu_const = 0.7978845608028654
beta_one = 0.9
beta_two = 0.95
learn_rate = 0.01
decay_rate = 0.1
adam_epsilon = 1e-08
step_count = 20

line = 4
groups = 2
pieces = 4
streams = 2


def gelu_tanh(value):
    inner = value * (gelu_const + (gelu_const * 0.044715) * (value * value))
    half = 0.5 * value
    return half + half * jnp.tanh(inner)


def gelu_slope(value):
    square = value * value
    tangent = jnp.tanh(value * (gelu_const + (gelu_const * 0.044715) * square))
    return 0.5 * (1.0 + tangent) + value * (1.0 - tangent * tangent) * (
        0.5 * gelu_const + (1.5 * gelu_const * 0.044715) * square
    )


def dot32(left, right):
    return jnp.dot(left, right, preferred_element_type=jnp.float32)


def route(patches, row_count, target_group, target_offset, block_rows):
    model_count, batch_count = lax.axis_size("mp"), lax.axis_size("dp")
    inner = batch_count // line
    devices_all = batch_count * model_count
    columns_all = inner * model_count
    slot_total, patch_width = patches.shape
    capacity = slot_total // devices_all
    lot = capacity + 1
    occupied = jnp.arange(slot_total, dtype=jnp.int32) < row_count[0]
    column = target_group % inner * model_count + target_offset // block_rows
    owner = jnp.where(occupied, column * line + target_group // inner, devices_all)
    onehot = (owner[:, None] == jnp.arange(devices_all, dtype=jnp.int32)[None, :]).astype(
        jnp.int32
    )
    placing = jnp.sum(onehot * jnp.cumsum(onehot, axis=0), axis=1) - 1
    slot = jnp.where(occupied, owner * lot + placing, devices_all * lot)
    spread = (jnp.arange(devices_all * lot, dtype=jnp.int32)[:, None] == slot[None, :]).astype(
        jnp.bfloat16
    )
    rows = dot32(spread, patches).astype(jnp.bfloat16).reshape(devices_all, lot, patch_width)
    lanes = (placing[:, None] == jnp.arange(patch_width, dtype=jnp.int32)[None, :]).astype(
        jnp.bfloat16
    )
    shifted = onehot * (target_offset % block_rows - block_rows)[:, None]
    marks = block_rows + lax.dot_general(
        shifted.astype(jnp.bfloat16),
        lanes,
        (((0,), (0,)), ((), ())),
        preferred_element_type=jnp.float32,
    )
    last = lax.broadcasted_iota(jnp.int32, rows.shape, 1) == capacity
    outgoing = jnp.where(last, marks.astype(jnp.bfloat16)[:, None, :], rows)
    outgoing = outgoing.reshape(1, columns_all, line * lot, patch_width)
    outgoing = jnp.broadcast_to(outgoing, (line,) + outgoing.shape[1:])
    arrived = lax.all_to_all(
        outgoing.reshape(devices_all, line * lot, patch_width),
        ("dp", "mp"),
        split_axis=0,
        concat_axis=0,
        tiled=True,
    )
    places = arrived.reshape(devices_all, line, lot, patch_width)[:, :, capacity, :lot]
    places = places.astype(jnp.int32)
    offsets = jnp.arange(line, dtype=jnp.int32)[None, :, None] * block_rows
    places = jnp.where(places < block_rows, places + offsets, line * block_rows)
    gather = (
        places.reshape(1, devices_all * line * lot)
        == jnp.arange(line * block_rows, dtype=jnp.int32)[:, None]
    ).astype(jnp.bfloat16)
    return dot32(gather, arrived.reshape(devices_all * line * lot, patch_width)).astype(
        jnp.bfloat16
    )


def adam_kernel(own_ref, came_ref, master_ref, moment1_ref, moment2_ref, *refs):
    master_out, moment1_out, moment2_out, copy_out = refs[-4:]
    gradient = own_ref[...] + came_ref[...].astype(jnp.float32)
    moment1_new = beta_one * moment1_ref[...] + (1.0 - beta_one) * gradient
    moment2_new = beta_two * moment2_ref[...] + (1.0 - beta_two) * gradient * gradient
    first_fix = moment1_new / (1.0 - beta_one**step_count)
    second_fix = moment2_new / (1.0 - beta_two**step_count)
    master = master_ref[...]
    master_new = master - learn_rate * (
        first_fix / (jnp.sqrt(second_fix) + adam_epsilon) + decay_rate * master
    )
    master_out[...] = master_new
    moment1_out[...] = moment1_new
    moment2_out[...] = moment2_new
    copy_out[...] = master_new.astype(jnp.bfloat16)


def adam_piece(own, came, state, outs, which):
    depth, cut = own.shape
    tile = depth // 3
    piece = pl.BlockSpec((tile, cut), lambda i: (i, 0))
    column = pl.BlockSpec((tile, cut), lambda i: (i, which))
    whole = [jax.ShapeDtypeStruct(state[0].shape, jnp.float32)] * 3
    whole.append(jax.ShapeDtypeStruct(state[0].shape, jnp.bfloat16))
    outs = outs or []
    return pl.pallas_call(
        adam_kernel,
        grid=(3,),
        in_specs=[piece, piece, column, column, column]
        + [pl.BlockSpec(memory_space=pl.ANY)] * len(outs),
        out_specs=[column] * 4,
        out_shape=whole,
        input_output_aliases={5 + i: i for i in range(len(outs))},
        compiler_params=pltpu.CompilerParams(vmem_limit_bytes=24 * 1024 * 1024),
        cost_estimate=pl.CostEstimate(
            flops=20 * depth * cut, bytes_accessed=32 * depth * cut, transcendentals=depth * cut
        ),
        name="adam_piece",
    )(own, came, *state, *outs)


def shards(
    patches,
    row_count,
    target_group,
    target_offset,
    embed,
    norm_gain,
    readout,
    target,
    master,
    moment1,
    moment2,
):
    model_count, batch_count = lax.axis_size("mp"), lax.axis_size("dp")
    inner = batch_count // line
    place = lax.axis_index("dp") // inner
    inside = lax.axis_index("dp") % inner
    last = line - 1
    at_end = (place == 0) | (place == last)
    far_side = place >= line // 2
    batch_rows = target.shape[0]
    block_rows = batch_rows // model_count
    width = embed.shape[1]
    patch_width = embed.shape[0]
    depth, columns = master.shape
    width_scale = 1.0 / width**0.5

    def swap(value, partners):
        pairs = [
            (p * inner + q, r * inner + q)
            for one, two in partners
            for p, r in ((one, two), (two, one))
            for q in range(inner)
        ]
        return lax.ppermute(value, "dp", pairs)

    def swap_end(value):
        return swap(value, ((0, 1), (last - 1, last)))

    def swap_middle(value):
        return swap(value, ((1, 2),))

    def turn(value, step):
        pairs = [
            (p * inner + q, p * inner + (q + step) % inner)
            for p in range(line)
            for q in range(inner)
        ]
        return lax.ppermute(value, "dp", pairs)

    def mp_sum(value, kind):
        step = 1
        while step < model_count:
            value = value.astype(kind)
            other = lax.ppermute(value, "mp", [(m, m ^ step) for m in range(model_count)])
            value = value.astype(jnp.float32) + other.astype(jnp.float32)
            step *= 2
        return value

    cut = columns // pieces
    lot = pieces // 2
    slices = [slice(piece * cut, (piece + 1) * cut) for piece in range(pieces)]
    weight_own = [
        master[:, first * cut : (first + lot) * cut].astype(jnp.bfloat16)
        for first in range(0, pieces, lot)
    ]
    weight_own[0], patches, target_offset = lax.optimization_barrier(
        (weight_own[0], patches, target_offset)
    )
    weight = []

    def gather_weight():
        rows = weight_own[len(weight)]
        if weight:
            rows, weight[-1] = lax.optimization_barrier((rows, weight[-1]))
        weight.append([rows] + [turn(rows, -step) for step in range(1, inner)])

    gather_weight()
    target_other = swap_end(target)

    blocks = route(patches, row_count, target_group, target_offset, block_rows)
    batches = lax.all_gather(blocks.reshape(line, block_rows, -1), "mp", axis=1, tiled=True)
    outbound = [jnp.where(far_side, batches[g], batches[last - g]) for g in range(groups)]
    inbound = [jnp.where(far_side, batches[last - g], batches[g]) for g in range(groups)]

    starts = [(place * inner + (inside + step) % inner) * depth for step in range(inner)]
    embed_here = jnp.concatenate(
        [lax.dynamic_slice_in_dim(embed, start, depth, axis=1) for start in starts], axis=1
    )
    gain_here = jnp.concatenate(
        [lax.dynamic_slice_in_dim(norm_gain, start, depth, axis=0) for start in starts], axis=0
    ).astype(jnp.float32)

    def make_features(tokens):
        return (gelu_tanh(dot32(tokens, embed_here)) * gain_here).astype(jnp.bfloat16)

    def local_scales():
        share = lax.axis_index("mp") * block_rows
        mine = jnp.concatenate(
            [lax.dynamic_slice_in_dim(tokens, share, block_rows, axis=0) for tokens in inbound],
            axis=0,
        )
        hidden = gelu_tanh(dot32(mine, embed))
        return lax.rsqrt(jnp.mean(hidden * hidden, axis=-1) + 1e-05) * width_scale

    def all_scales(scale):
        placed = jnp.zeros((groups, model_count, block_rows), jnp.float32)
        placed = lax.dynamic_update_slice_in_dim(
            placed, scale.reshape(groups, 1, block_rows), lax.axis_index("mp"), axis=1
        )
        placed = mp_sum(placed.reshape(groups, batch_rows), jnp.float32)
        return [placed[g][:, None] for g in range(groups)]

    units = groups * pieces
    goals = [target, target_other]
    rows_each = batch_rows // streams
    parts = [slice(part * rows_each, (part + 1) * rows_each) for part in range(streams)]
    features, scales, predicted, errors = [], [], [], []
    sums, preact, delta = {}, {}, {}
    ends, middles = {}, {}
    early, pending, outs = {}, {}, None

    def wide(value):
        return value.astype(jnp.float32)

    def group_features(group):
        return make_features(jnp.concatenate([outbound[group], inbound[group]], axis=0))

    joined = {}

    def partial_sums(group, side, which):
        if which not in joined:
            joined[which] = jnp.concatenate(weight[which], axis=0)
        left = features[group][side * batch_rows :][:batch_rows]
        return dot32(left, joined[which]).astype(jnp.bfloat16)

    def sums_of(unit, side, rows=slice(None)):
        group, piece = divmod(unit, pieces)
        return sums[group, side, piece // lot][rows, slices[piece % lot]]

    def finished(unit, before):
        group, piece = divmod(unit, pieces)
        value = (wide(sums_of(unit, 1)) + wide(before)) * scales[group]
        active = gelu_tanh(value).astype(jnp.bfloat16)
        return value, dot32(active, readout[slices[piece]])

    def new_delta(part, unit, before):
        group, piece = divmod(unit, pieces)
        back = lax.dot_general(
            lax.optimization_barrier((errors[group][parts[part]], before))[0],
            readout[slices[piece]],
            (((1,), (1,)), ((), ())),
            preferred_element_type=jnp.float32,
        )
        slope = gelu_slope(preact[unit][parts[part]])
        return (back * slope * scales[group][parts[part]]).astype(jnp.bfloat16)

    def gradient_term(unit, rows):
        first = units + unit
        arrived = [
            jnp.where(at_end, ends[part, first + 2], middles[part, first + 1])
            for part in range(streams)
        ] + [jnp.where(at_end, delta[part, unit], ends[part, first]) for part in range(streams)]
        return lax.dot_general(
            features[unit // pieces][:, rows],
            jnp.concatenate(arrived, axis=0),
            (((0,), (0,)), ((), ())),
            preferred_element_type=jnp.float32,
        )

    features.append(group_features(0))
    sums[0, 0, 0] = partial_sums(0, 0, 0)
    gather_weight()
    late = streams - 1
    side_work = {
        (0, 0): [(0, 1, 0), "scales", "features"],
        (0, late): [(1, 0, 0), (1, 1, 0)],
        (1, late): [(0, 0, 1)],
        (2, late): [(0, 1, 1)],
        (3, late): [(1, 0, 1)],
        (4, late): [(1, 1, 1)],
    }
    for tick, part in [(t, p) for t in range(2 * units + line) for p in range(streams)]:
        back_tick = tick - units
        was_end = was_middle = None
        if tick:
            was_end, was_middle, pending = lax.optimization_barrier(
                (ends.get((part, tick - 1)), middles.get((part, tick - 1)), pending)
            )
            ends[part, tick - 1], middles[part, tick - 1] = was_end, was_middle
            for box, key in list(pending):
                value = pending.pop((box, key))
                if box == "sums":
                    sums[key] = value
                elif box == "delta":
                    delta[key] = value
                elif box == "early":
                    early[key] = value
                else:
                    scales = all_scales(value)

        from_end = from_middle = None
        if tick < units:
            from_end = sums_of(tick, 0, parts[part])
        elif back_tick < units:
            from_end = delta[part, back_tick]
        elif back_tick == units:
            narrow = predicted[1][parts[part]].astype(jnp.bfloat16)
            from_end = jnp.pad(narrow, ((0, 0), (0, cut - patch_width)))
        if 2 <= tick < units + 2:
            from_middle = (wide(sums_of(tick - 2, 1, parts[part])) + wide(was_middle)).astype(jnp.bfloat16)
        elif 2 <= back_tick < units + 2:
            from_middle = was_middle
        if from_end is None or from_middle is None:
            payload = from_middle if from_end is None else from_end
        else:
            payload = jnp.where(at_end, from_end, from_middle)
        if payload is not None:
            ends[part, tick] = swap_end(payload)
        if 1 <= tick < units + 1:
            payload = (wide(sums_of(tick - 1, 0, parts[part])) + wide(was_end)).astype(jnp.bfloat16)
            middles[part, tick] = swap_middle(payload)
        elif 1 <= back_tick < units + 1:
            middles[part, tick] = swap_middle(was_end)

        for work in side_work.get((tick, part), ()):
            if work == "scales":
                pending["scales", None] = local_scales()
            elif work == "features":
                features.append(group_features(1))
            else:
                group = work[0]
                if tick > 1:
                    features[group] = lax.optimization_barrier((features[group], was_end))[0]
                pending["sums", work] = partial_sums(*work)

        group, piece = divmod(tick - line + 1, pieces)
        if 0 <= group < groups and piece == pieces - 1 and part == late:
            total = 0.0
            for unit in range(group * pieces, (group + 1) * pieces):
                arrived = [ends[other, unit + 2] for other in range(streams)]
                preact[unit], value = finished(unit, jnp.concatenate(arrived, axis=0))
                total += value
            predicted.append(mp_sum(total, jnp.bfloat16))
            errors.append((predicted[-1] - wide(goals[group])).astype(jnp.bfloat16))

        unit = back_tick + 1
        if 0 <= unit < units:
            value = new_delta(part, unit, was_end)
            if unit % pieces:
                pending["delta", (part, unit)] = value
            else:
                delta[part, unit] = value

        unit = back_tick - line + 1
        if 0 <= unit < units and part == streams - 1:
            group, piece = divmod(unit, pieces)
            if group < groups - 1:
                pending["early", (group, piece)] = gradient_term(unit, slice(None))
            else:
                total = None
                for step in [*range(1, inner), 0]:
                    rows = slice(step * depth, (step + 1) * depth)
                    value = gradient_term(unit, rows)
                    for other in range(groups - 1):
                        value += early[other, piece][rows]
                    if step == 0:
                        outs = adam_piece(value, total, (master, moment1, moment2), outs, piece)
                    else:
                        value = turn(value.astype(jnp.bfloat16), step)
                        total = value if total is None else (wide(total) + wide(value)).astype(
                            jnp.bfloat16
                        )

    from_ends = [ends[part, 2 * units][:, :patch_width] for part in range(streams)]
    prediction = jnp.where(at_end, predicted[0], wide(jnp.concatenate(from_ends, axis=0)))
    return (prediction, *outs)


def solution(mesh):
    placed = (
        P(("dp", "mp"), None),
        P(("dp", "mp")),
        P(("dp", "mp")),
        P(("dp", "mp")),
        P(),
        P(),
        P("mp", None),
        P("dp", None),
        P("dp", "mp"),
        P("dp", "mp"),
        P("dp", "mp"),
    )
    return jax.shard_map(
        shards,
        mesh=mesh,
        in_specs=placed,
        out_specs=(P("dp", None), P("dp", "mp"), P("dp", "mp"), P("dp", "mp"), P("dp", "mp")),
        check_vma=False,
    )
```

```python
import jax
import jax.numpy as jnp
from jax import lax
from jax.experimental import pallas as pl
from jax.experimental.pallas import tpu as pltpu
from jax.sharding import PartitionSpec as P

gelu_const = 0.7978845608028654
beta_one = 0.9
beta_two = 0.95
learn_rate = 0.01
decay_rate = 0.1
adam_epsilon = 1e-08
step_count = 20

line = 4
groups = 2
pieces = 4
streams = 2


def gelu_tanh(value):
    inner = value * (gelu_const + (gelu_const * 0.044715) * (value * value))
    half = 0.5 * value
    return half + half * jnp.tanh(inner)


def gelu_slope(value):
    square = value * value
    tangent = jnp.tanh(value * (gelu_const + (gelu_const * 0.044715) * square))
    return 0.5 * (1.0 + tangent) + value * (1.0 - tangent * tangent) * (
        0.5 * gelu_const + (1.5 * gelu_const * 0.044715) * square
    )


def dot32(left, right):
    return jnp.dot(left, right, preferred_element_type=jnp.float32)


def route(patches, row_count, target_group, target_offset, block_rows):
    model_count, batch_count = lax.axis_size("mp"), lax.axis_size("dp")
    inner = batch_count // line
    devices_all = batch_count * model_count
    columns_all = inner * model_count
    slot_total, patch_width = patches.shape
    capacity = slot_total // devices_all
    lot = capacity + 1
    occupied = jnp.arange(slot_total, dtype=jnp.int32) < row_count[0]
    column = target_group % inner * model_count + target_offset // block_rows
    owner = jnp.where(occupied, column * line + target_group // inner, devices_all)
    onehot = (owner[:, None] == jnp.arange(devices_all, dtype=jnp.int32)[None, :]).astype(
        jnp.int32
    )
    placing = jnp.sum(onehot * jnp.cumsum(onehot, axis=0), axis=1) - 1
    slot = jnp.where(occupied, owner * lot + placing, devices_all * lot)
    spread = (jnp.arange(devices_all * lot, dtype=jnp.int32)[:, None] == slot[None, :]).astype(
        jnp.bfloat16
    )
    rows = dot32(spread, patches).astype(jnp.bfloat16).reshape(devices_all, lot, patch_width)
    lanes = (placing[:, None] == jnp.arange(patch_width, dtype=jnp.int32)[None, :]).astype(
        jnp.bfloat16
    )
    shifted = onehot * (target_offset % block_rows - block_rows)[:, None]
    marks = block_rows + lax.dot_general(
        shifted.astype(jnp.bfloat16),
        lanes,
        (((0,), (0,)), ((), ())),
        preferred_element_type=jnp.float32,
    )
    last = lax.broadcasted_iota(jnp.int32, rows.shape, 1) == capacity
    outgoing = jnp.where(last, marks.astype(jnp.bfloat16)[:, None, :], rows)
    outgoing = outgoing.reshape(1, columns_all, line * lot, patch_width)
    outgoing = jnp.broadcast_to(outgoing, (line,) + outgoing.shape[1:])
    arrived = lax.all_to_all(
        outgoing.reshape(devices_all, line * lot, patch_width),
        ("dp", "mp"),
        split_axis=0,
        concat_axis=0,
        tiled=True,
    )
    places = arrived.reshape(devices_all, line, lot, patch_width)[:, :, capacity, :lot]
    places = places.astype(jnp.int32)
    offsets = jnp.arange(line, dtype=jnp.int32)[None, :, None] * block_rows
    places = jnp.where(places < block_rows, places + offsets, line * block_rows)
    gather = (
        places.reshape(1, devices_all * line * lot)
        == jnp.arange(line * block_rows, dtype=jnp.int32)[:, None]
    ).astype(jnp.bfloat16)
    return dot32(gather, arrived.reshape(devices_all * line * lot, patch_width)).astype(
        jnp.bfloat16
    )


def adam_kernel(own_ref, came_ref, master_ref, moment1_ref, moment2_ref, *refs):
    master_out, moment1_out, moment2_out, copy_out = refs[-4:]
    gradient = own_ref[...] + came_ref[...].astype(jnp.float32)
    moment1_new = beta_one * moment1_ref[...] + (1.0 - beta_one) * gradient
    moment2_new = beta_two * moment2_ref[...] + (1.0 - beta_two) * gradient * gradient
    first_fix = moment1_new / (1.0 - beta_one**step_count)
    second_fix = moment2_new / (1.0 - beta_two**step_count)
    master = master_ref[...]
    master_new = master - learn_rate * (
        first_fix / (jnp.sqrt(second_fix) + adam_epsilon) + decay_rate * master
    )
    master_out[...] = master_new
    moment1_out[...] = moment1_new
    moment2_out[...] = moment2_new
    copy_out[...] = master_new.astype(jnp.bfloat16)


def adam_piece(own, came, state, outs, which):
    depth, cut = own.shape
    tile = depth // 3
    piece = pl.BlockSpec((tile, cut), lambda i: (i, 0))
    column = pl.BlockSpec((tile, cut), lambda i: (i, which))
    whole = [jax.ShapeDtypeStruct(state[0].shape, jnp.float32)] * 3
    whole.append(jax.ShapeDtypeStruct(state[0].shape, jnp.bfloat16))
    outs = outs or []
    return pl.pallas_call(
        adam_kernel,
        grid=(3,),
        in_specs=[piece, piece, column, column, column]
        + [pl.BlockSpec(memory_space=pl.ANY)] * len(outs),
        out_specs=[column] * 4,
        out_shape=whole,
        input_output_aliases={5 + i: i for i in range(len(outs))},
        compiler_params=pltpu.CompilerParams(vmem_limit_bytes=24 * 1024 * 1024),
        cost_estimate=pl.CostEstimate(
            flops=20 * depth * cut, bytes_accessed=32 * depth * cut, transcendentals=depth * cut
        ),
        name="adam_piece",
    )(own, came, *state, *outs)


def shards(
    patches,
    row_count,
    target_group,
    target_offset,
    embed,
    norm_gain,
    readout,
    target,
    master,
    moment1,
    moment2,
):
    model_count, batch_count = lax.axis_size("mp"), lax.axis_size("dp")
    inner = batch_count // line
    place = lax.axis_index("dp") // inner
    inside = lax.axis_index("dp") % inner
    last = line - 1
    at_end = (place == 0) | (place == last)
    far_side = place >= line // 2
    batch_rows = target.shape[0]
    block_rows = batch_rows // model_count
    width = embed.shape[1]
    patch_width = embed.shape[0]
    depth, columns = master.shape
    width_scale = 1.0 / width**0.5

    def swap(value, partners):
        pairs = [
            (p * inner + q, r * inner + q)
            for one, two in partners
            for p, r in ((one, two), (two, one))
            for q in range(inner)
        ]
        return lax.ppermute(value, "dp", pairs)

    def swap_end(value):
        return swap(value, ((0, 1), (last - 1, last)))

    def swap_middle(value):
        return swap(value, ((1, 2),))

    def turn(value, step):
        pairs = [
            (p * inner + q, p * inner + (q + step) % inner)
            for p in range(line)
            for q in range(inner)
        ]
        return lax.ppermute(value, "dp", pairs)

    def mp_sum(value, kind):
        step = 1
        while step < model_count:
            value = value.astype(kind)
            other = lax.ppermute(value, "mp", [(m, m ^ step) for m in range(model_count)])
            value = value.astype(jnp.float32) + other.astype(jnp.float32)
            step *= 2
        return value

    cut = columns // pieces
    lot = pieces // 2
    slices = [slice(piece * cut, (piece + 1) * cut) for piece in range(pieces)]
    weight_own = [
        master[:, first * cut : (first + lot) * cut].astype(jnp.bfloat16)
        for first in range(0, pieces, lot)
    ]
    weight_own[0], patches, target_offset = lax.optimization_barrier(
        (weight_own[0], patches, target_offset)
    )
    weight = []

    def gather_weight():
        rows = weight_own[len(weight)]
        if weight:
            rows, weight[-1] = lax.optimization_barrier((rows, weight[-1]))
        weight.append([rows] + [turn(rows, -step) for step in range(1, inner)])

    gather_weight()
    target_other = swap_end(target)

    blocks = route(patches, row_count, target_group, target_offset, block_rows)
    batches = lax.all_gather(blocks.reshape(line, block_rows, -1), "mp", axis=1, tiled=True)
    outbound = [jnp.where(far_side, batches[g], batches[last - g]) for g in range(groups)]
    inbound = [jnp.where(far_side, batches[last - g], batches[g]) for g in range(groups)]

    starts = [(place * inner + (inside + step) % inner) * depth for step in range(inner)]
    embed_here = jnp.concatenate(
        [lax.dynamic_slice_in_dim(embed, start, depth, axis=1) for start in starts], axis=1
    )
    gain_here = jnp.concatenate(
        [lax.dynamic_slice_in_dim(norm_gain, start, depth, axis=0) for start in starts], axis=0
    ).astype(jnp.float32)

    def make_features(tokens):
        return (gelu_tanh(dot32(tokens, embed_here)) * gain_here).astype(jnp.bfloat16)

    def local_scales():
        share = lax.axis_index("mp") * block_rows
        mine = jnp.concatenate(
            [lax.dynamic_slice_in_dim(tokens, share, block_rows, axis=0) for tokens in inbound],
            axis=0,
        )
        hidden = gelu_tanh(dot32(mine, embed))
        return lax.rsqrt(jnp.mean(hidden * hidden, axis=-1) + 1e-05) * width_scale

    def all_scales(scale):
        placed = jnp.zeros((groups, model_count, block_rows), jnp.float32)
        placed = lax.dynamic_update_slice_in_dim(
            placed, scale.reshape(groups, 1, block_rows), lax.axis_index("mp"), axis=1
        )
        placed = mp_sum(placed.reshape(groups, batch_rows), jnp.float32)
        return [placed[g][:, None] for g in range(groups)]

    units = groups * pieces
    goals = [target, target_other]
    rows_each = batch_rows // streams
    parts = [slice(part * rows_each, (part + 1) * rows_each) for part in range(streams)]
    features, scales, predicted, errors = [], [], [], []
    sums, preact, delta = {}, {}, {}
    ends, middles = {}, {}
    early, pending, outs = {}, {}, None

    def wide(value):
        return value.astype(jnp.float32)

    def group_features(group):
        return make_features(jnp.concatenate([outbound[group], inbound[group]], axis=0))

    joined = {}

    def partial_sums(group, side, which):
        if which not in joined:
            joined[which] = jnp.concatenate(weight[which], axis=0)
        left = features[group][side * batch_rows :][:batch_rows]
        return dot32(left, joined[which]).astype(jnp.bfloat16)

    def sums_of(unit, side, rows=slice(None)):
        group, piece = divmod(unit, pieces)
        return sums[group, side, piece // lot][rows, slices[piece % lot]]

    def finished(unit, before):
        group, piece = divmod(unit, pieces)
        value = (wide(sums_of(unit, 1)) + wide(before)) * scales[group]
        active = gelu_tanh(value).astype(jnp.bfloat16)
        return value, dot32(active, readout[slices[piece]])

    def new_delta(part, unit, before):
        group, piece = divmod(unit, pieces)
        back = lax.dot_general(
            lax.optimization_barrier((errors[group][parts[part]], before))[0],
            readout[slices[piece]],
            (((1,), (1,)), ((), ())),
            preferred_element_type=jnp.float32,
        )
        slope = gelu_slope(preact[unit][parts[part]])
        return (back * slope * scales[group][parts[part]]).astype(jnp.bfloat16)

    def gradient_term(unit, rows):
        first = units + unit
        arrived = [
            jnp.where(at_end, ends[part, first + 2], middles[part, first + 1])
            for part in range(streams)
        ] + [jnp.where(at_end, delta[part, unit], ends[part, first]) for part in range(streams)]
        return lax.dot_general(
            features[unit // pieces][:, rows],
            jnp.concatenate(arrived, axis=0),
            (((0,), (0,)), ((), ())),
            preferred_element_type=jnp.float32,
        )

    features.append(group_features(0))
    sums[0, 0, 0] = partial_sums(0, 0, 0)
    gather_weight()
    late = streams - 1
    side_work = {
        (0, 0): [(0, 1, 0), "scales", "features"],
        (0, late): [(1, 0, 0), (1, 1, 0)],
        (1, late): [(0, 0, 1)],
        (2, 0): [(0, 1, 1)],
        (2, late): [(1, 0, 1), (1, 1, 1)],
    }
    for tick, part in [(t, p) for t in range(2 * units + line) for p in range(streams)]:
        back_tick = tick - units
        was_end = was_middle = None
        if tick:
            was_end, was_middle, pending = lax.optimization_barrier(
                (ends.get((part, tick - 1)), middles.get((part, tick - 1)), pending)
            )
            ends[part, tick - 1], middles[part, tick - 1] = was_end, was_middle
            for box, key in list(pending):
                value = pending.pop((box, key))
                if box == "sums":
                    sums[key] = value
                elif box == "delta":
                    delta[key] = value
                elif box == "early":
                    early[key] = value
                elif box == "scales":
                    scales = all_scales(value)

        from_end = from_middle = None
        if tick < units:
            from_end = sums_of(tick, 0, parts[part])
        elif back_tick < units:
            from_end = delta[part, back_tick]
        elif back_tick == units:
            narrow = predicted[1][parts[part]].astype(jnp.bfloat16)
            from_end = jnp.pad(narrow, ((0, 0), (0, cut - patch_width)))
        if 2 <= tick < units + 2:
            from_middle = (wide(sums_of(tick - 2, 1, parts[part])) + wide(was_middle)).astype(jnp.bfloat16)
        elif 2 <= back_tick < units + 2:
            from_middle = was_middle
        if from_end is None or from_middle is None:
            payload = from_middle if from_end is None else from_end
        else:
            payload = jnp.where(at_end, from_end, from_middle)
        if payload is not None:
            if tick < units + 2:
                pending["sent", "end"] = payload
            ends[part, tick] = swap_end(payload)
        if 1 <= tick < units + 1:
            payload = (wide(sums_of(tick - 1, 0, parts[part])) + wide(was_end)).astype(jnp.bfloat16)
            middles[part, tick] = swap_middle(payload)
        elif 1 <= back_tick < units + 1:
            middles[part, tick] = swap_middle(was_end)

        if payload is not None and tick < 99:
            pending["sent", "last"] = payload
        for work in side_work.get((tick, part), ()):
            if work == "scales":
                pending["scales", None] = local_scales()
            elif work == "features":
                features.append(group_features(1))
            else:
                group = work[0]
                if tick > 1:
                    features[group] = lax.optimization_barrier((features[group], was_end))[0]
                pending["sums", work] = partial_sums(*work)

        group, piece = divmod(tick - line + 1, pieces)
        if 0 <= group < groups and piece == pieces - 1 and part == late:
            total = 0.0
            for unit in range(group * pieces, (group + 1) * pieces):
                arrived = [ends[other, unit + 2] for other in range(streams)]
                preact[unit], value = finished(unit, jnp.concatenate(arrived, axis=0))
                total += value
            predicted.append(mp_sum(total, jnp.bfloat16))
            errors.append((predicted[-1] - wide(goals[group])).astype(jnp.bfloat16))

        unit = back_tick + 1
        if 0 <= unit < units:
            pending["delta", (part, unit)] = new_delta(part, unit, was_end)

        unit = back_tick - line + 1
        if 0 <= unit < units and part == streams - 1:
            group, piece = divmod(unit, pieces)
            if group < groups - 1:
                pending["early", (group, piece)] = gradient_term(unit, slice(None))
            else:
                total = None
                for step in [*range(1, inner), 0]:
                    rows = slice(step * depth, (step + 1) * depth)
                    value = gradient_term(unit, rows)
                    for other in range(groups - 1):
                        value += early[other, piece][rows]
                    if step == 0:
                        outs = adam_piece(value, total, (master, moment1, moment2), outs, piece)
                    else:
                        value = turn(value.astype(jnp.bfloat16), step)
                        total = value if total is None else (wide(total) + wide(value)).astype(
                            jnp.bfloat16
                        )

    from_ends = [ends[part, 2 * units][:, :patch_width] for part in range(streams)]
    prediction = jnp.where(at_end, predicted[0], wide(jnp.concatenate(from_ends, axis=0)))
    return (prediction, *outs)


def solution(mesh):
    placed = (
        P(("dp", "mp"), None),
        P(("dp", "mp")),
        P(("dp", "mp")),
        P(("dp", "mp")),
        P(),
        P(),
        P("mp", None),
        P("dp", None),
        P("dp", "mp"),
        P("dp", "mp"),
        P("dp", "mp"),
    )
    return jax.shard_map(
        shards,
        mesh=mesh,
        in_specs=placed,
        out_specs=(P("dp", None), P("dp", "mp"), P("dp", "mp"), P("dp", "mp"), P("dp", "mp")),
        check_vma=False,
    )
```

```python
import jax
import jax.numpy as jnp
from jax import lax
from jax.experimental import pallas as pl
from jax.experimental.pallas import tpu as pltpu
from jax.sharding import PartitionSpec as P

gelu_const = 0.7978845608028654
beta_one = 0.9
beta_two = 0.95
learn_rate = 0.01
decay_rate = 0.1
adam_epsilon = 1e-08
step_count = 20

line = 4
groups = 2
pieces = 4
streams = 2


def gelu_tanh(value):
    inner = value * (gelu_const + (gelu_const * 0.044715) * (value * value))
    half = 0.5 * value
    return half + half * jnp.tanh(inner)


def gelu_slope(value):
    square = value * value
    tangent = jnp.tanh(value * (gelu_const + (gelu_const * 0.044715) * square))
    return 0.5 * (1.0 + tangent) + value * (1.0 - tangent * tangent) * (
        0.5 * gelu_const + (1.5 * gelu_const * 0.044715) * square
    )


def dot32(left, right):
    return jnp.dot(left, right, preferred_element_type=jnp.float32)


def route(patches, row_count, target_group, target_offset, block_rows):
    model_count, batch_count = lax.axis_size("mp"), lax.axis_size("dp")
    inner = batch_count // line
    devices_all = batch_count * model_count
    columns_all = inner * model_count
    slot_total, patch_width = patches.shape
    capacity = slot_total // devices_all
    lot = capacity + 1
    occupied = jnp.arange(slot_total, dtype=jnp.int32) < row_count[0]
    column = target_group % inner * model_count + target_offset // block_rows
    owner = jnp.where(occupied, column * line + target_group // inner, devices_all)
    onehot = (owner[:, None] == jnp.arange(devices_all, dtype=jnp.int32)[None, :]).astype(
        jnp.int32
    )
    placing = jnp.sum(onehot * jnp.cumsum(onehot, axis=0), axis=1) - 1
    slot = jnp.where(occupied, owner * lot + placing, devices_all * lot)
    spread = (jnp.arange(devices_all * lot, dtype=jnp.int32)[:, None] == slot[None, :]).astype(
        jnp.bfloat16
    )
    rows = dot32(spread, patches).astype(jnp.bfloat16).reshape(devices_all, lot, patch_width)
    lanes = (placing[:, None] == jnp.arange(patch_width, dtype=jnp.int32)[None, :]).astype(
        jnp.bfloat16
    )
    shifted = onehot * (target_offset % block_rows - block_rows)[:, None]
    marks = block_rows + lax.dot_general(
        shifted.astype(jnp.bfloat16),
        lanes,
        (((0,), (0,)), ((), ())),
        preferred_element_type=jnp.float32,
    )
    last = lax.broadcasted_iota(jnp.int32, rows.shape, 1) == capacity
    outgoing = jnp.where(last, marks.astype(jnp.bfloat16)[:, None, :], rows)
    outgoing = outgoing.reshape(1, columns_all, line * lot, patch_width)
    outgoing = jnp.broadcast_to(outgoing, (line,) + outgoing.shape[1:])
    arrived = lax.all_to_all(
        outgoing.reshape(devices_all, line * lot, patch_width),
        ("dp", "mp"),
        split_axis=0,
        concat_axis=0,
        tiled=True,
    )
    places = arrived.reshape(devices_all, line, lot, patch_width)[:, :, capacity, :lot]
    places = places.astype(jnp.int32)
    offsets = jnp.arange(line, dtype=jnp.int32)[None, :, None] * block_rows
    places = jnp.where(places < block_rows, places + offsets, line * block_rows)
    gather = (
        places.reshape(1, devices_all * line * lot)
        == jnp.arange(line * block_rows, dtype=jnp.int32)[:, None]
    ).astype(jnp.bfloat16)
    return dot32(gather, arrived.reshape(devices_all * line * lot, patch_width)).astype(
        jnp.bfloat16
    )


def adam_kernel(own_ref, came_ref, master_ref, moment1_ref, moment2_ref, *refs):
    master_out, moment1_out, moment2_out, copy_out = refs[-4:]
    gradient = own_ref[...] + came_ref[...].astype(jnp.float32)
    moment1_new = beta_one * moment1_ref[...] + (1.0 - beta_one) * gradient
    moment2_new = beta_two * moment2_ref[...] + (1.0 - beta_two) * gradient * gradient
    first_fix = moment1_new / (1.0 - beta_one**step_count)
    second_fix = moment2_new / (1.0 - beta_two**step_count)
    master = master_ref[...]
    master_new = master - learn_rate * (
        first_fix / (jnp.sqrt(second_fix) + adam_epsilon) + decay_rate * master
    )
    master_out[...] = master_new
    moment1_out[...] = moment1_new
    moment2_out[...] = moment2_new
    copy_out[...] = master_new.astype(jnp.bfloat16)


def adam_piece(own, came, state, outs, which):
    depth, cut = own.shape
    tile = depth // 3
    piece = pl.BlockSpec((tile, cut), lambda i: (i, 0))
    column = pl.BlockSpec((tile, cut), lambda i: (i, which))
    whole = [jax.ShapeDtypeStruct(state[0].shape, jnp.float32)] * 3
    whole.append(jax.ShapeDtypeStruct(state[0].shape, jnp.bfloat16))
    outs = outs or []
    return pl.pallas_call(
        adam_kernel,
        grid=(3,),
        in_specs=[piece, piece, column, column, column]
        + [pl.BlockSpec(memory_space=pl.ANY)] * len(outs),
        out_specs=[column] * 4,
        out_shape=whole,
        input_output_aliases={5 + i: i for i in range(len(outs))},
        compiler_params=pltpu.CompilerParams(vmem_limit_bytes=24 * 1024 * 1024),
        cost_estimate=pl.CostEstimate(
            flops=20 * depth * cut, bytes_accessed=32 * depth * cut, transcendentals=depth * cut
        ),
        name="adam_piece",
    )(own, came, *state, *outs)


def shards(
    patches,
    row_count,
    target_group,
    target_offset,
    embed,
    norm_gain,
    readout,
    target,
    master,
    moment1,
    moment2,
):
    model_count, batch_count = lax.axis_size("mp"), lax.axis_size("dp")
    inner = batch_count // line
    place = lax.axis_index("dp") // inner
    inside = lax.axis_index("dp") % inner
    last = line - 1
    at_end = (place == 0) | (place == last)
    far_side = place >= line // 2
    batch_rows = target.shape[0]
    block_rows = batch_rows // model_count
    width = embed.shape[1]
    patch_width = embed.shape[0]
    depth, columns = master.shape
    width_scale = 1.0 / width**0.5

    def swap(value, partners):
        pairs = [
            (p * inner + q, r * inner + q)
            for one, two in partners
            for p, r in ((one, two), (two, one))
            for q in range(inner)
        ]
        return lax.ppermute(value, "dp", pairs)

    def swap_end(value):
        return swap(value, ((0, 1), (last - 1, last)))

    def swap_middle(value):
        return swap(value, ((1, 2),))

    def turn(value, step):
        pairs = [
            (p * inner + q, p * inner + (q + step) % inner)
            for p in range(line)
            for q in range(inner)
        ]
        return lax.ppermute(value, "dp", pairs)

    def mp_sum(value, kind):
        step = 1
        while step < model_count:
            value = value.astype(kind)
            other = lax.ppermute(value, "mp", [(m, m ^ step) for m in range(model_count)])
            value = value.astype(jnp.float32) + other.astype(jnp.float32)
            step *= 2
        return value

    cut = columns // pieces
    lot = pieces // 2
    slices = [slice(piece * cut, (piece + 1) * cut) for piece in range(pieces)]
    weight_own = [
        master[:, first * cut : (first + lot) * cut].astype(jnp.bfloat16)
        for first in range(0, pieces, lot)
    ]
    weight_own[0], patches, target_offset = lax.optimization_barrier(
        (weight_own[0], patches, target_offset)
    )
    weight = []

    def gather_weight():
        rows = weight_own[len(weight)]
        if weight:
            rows, weight[-1] = lax.optimization_barrier((rows, weight[-1]))
        weight.append([rows] + [turn(rows, -step) for step in range(1, inner)])

    gather_weight()
    target_other = swap_end(target)

    blocks = route(patches, row_count, target_group, target_offset, block_rows)
    batches = lax.all_gather(blocks.reshape(line, block_rows, -1), "mp", axis=1, tiled=True)
    outbound = [jnp.where(far_side, batches[g], batches[last - g]) for g in range(groups)]
    inbound = [jnp.where(far_side, batches[last - g], batches[g]) for g in range(groups)]

    starts = [(place * inner + (inside + step) % inner) * depth for step in range(inner)]
    embed_here = jnp.concatenate(
        [lax.dynamic_slice_in_dim(embed, start, depth, axis=1) for start in starts], axis=1
    )
    gain_here = jnp.concatenate(
        [lax.dynamic_slice_in_dim(norm_gain, start, depth, axis=0) for start in starts], axis=0
    ).astype(jnp.float32)

    def make_features(tokens):
        return (gelu_tanh(dot32(tokens, embed_here)) * gain_here).astype(jnp.bfloat16)

    def local_scales():
        share = lax.axis_index("mp") * block_rows
        mine = jnp.concatenate(
            [lax.dynamic_slice_in_dim(tokens, share, block_rows, axis=0) for tokens in inbound],
            axis=0,
        )
        hidden = gelu_tanh(dot32(mine, embed))
        return lax.rsqrt(jnp.mean(hidden * hidden, axis=-1) + 1e-05) * width_scale

    def all_scales(scale):
        placed = jnp.zeros((groups, model_count, block_rows), jnp.float32)
        placed = lax.dynamic_update_slice_in_dim(
            placed, scale.reshape(groups, 1, block_rows), lax.axis_index("mp"), axis=1
        )
        placed = mp_sum(placed.reshape(groups, batch_rows), jnp.float32)
        return [placed[g][:, None] for g in range(groups)]

    units = groups * pieces
    goals = [target, target_other]
    rows_each = batch_rows // streams
    parts = [slice(part * rows_each, (part + 1) * rows_each) for part in range(streams)]
    features, scales, predicted, errors = [], [], [], []
    sums, preact, delta = {}, {}, {}
    ends, middles = {}, {}
    early, pending, outs = {}, {}, None

    def wide(value):
        return value.astype(jnp.float32)

    def group_features(group):
        return make_features(jnp.concatenate([outbound[group], inbound[group]], axis=0))

    joined, own_sums = {}, {}

    def partial_sums(group, side, which):
        if (group, side, which) in own_sums:
            value = own_sums[group, side, which]
            for step in range(1, inner):
                rows = slice(step * depth, (step + 1) * depth)
                left = features[group][side * batch_rows :][:batch_rows, rows]
                value += dot32(left, weight[which][step])
            return value.astype(jnp.bfloat16)
        if which not in joined:
            joined[which] = jnp.concatenate(weight[which], axis=0)
        left = features[group][side * batch_rows :][:batch_rows]
        return dot32(left, joined[which]).astype(jnp.bfloat16)

    def sums_of(unit, side, rows=slice(None)):
        group, piece = divmod(unit, pieces)
        return sums[group, side, piece // lot][rows, slices[piece % lot]]

    def finished(unit, before):
        group, piece = divmod(unit, pieces)
        value = (wide(sums_of(unit, 1)) + wide(before)) * scales[group]
        active = gelu_tanh(value).astype(jnp.bfloat16)
        return value, dot32(active, readout[slices[piece]])

    def new_delta(part, unit, before):
        group, piece = divmod(unit, pieces)
        back = lax.dot_general(
            lax.optimization_barrier((errors[group][parts[part]], before))[0],
            readout[slices[piece]],
            (((1,), (1,)), ((), ())),
            preferred_element_type=jnp.float32,
        )
        slope = gelu_slope(preact[unit][parts[part]])
        return (back * slope * scales[group][parts[part]]).astype(jnp.bfloat16)

    def gradient_term(unit, rows):
        first = units + unit
        arrived = [
            jnp.where(at_end, ends[part, first + 2], middles[part, first + 1])
            for part in range(streams)
        ] + [jnp.where(at_end, delta[part, unit], ends[part, first]) for part in range(streams)]
        return lax.dot_general(
            features[unit // pieces][:, rows],
            jnp.concatenate(arrived, axis=0),
            (((0,), (0,)), ((), ())),
            preferred_element_type=jnp.float32,
        )

    features.append(group_features(0))
    sums[0, 0, 0] = partial_sums(0, 0, 0)
    gather_weight()
    late = streams - 1
    side_work = {
        (0, 0): [(0, 1, 0), "scales", "features"],
        (0, late): [(1, 0, 0), (1, 1, 0), "own"],
        (1, late): [(0, 0, 1)],
        (2, 0): [(0, 1, 1)],
        (2, late): [(1, 0, 1), (1, 1, 1)],
    }
    for tick, part in [(t, p) for t in range(2 * units + line) for p in range(streams)]:
        back_tick = tick - units
        was_end = was_middle = None
        if tick:
            was_end, was_middle, pending = lax.optimization_barrier(
                (ends.get((part, tick - 1)), middles.get((part, tick - 1)), pending)
            )
            ends[part, tick - 1], middles[part, tick - 1] = was_end, was_middle
            for box, key in list(pending):
                value = pending.pop((box, key))
                if box == "sums":
                    sums[key] = value
                elif box == "delta":
                    delta[key] = value
                elif box == "own":
                    own_sums[key] = value
                elif box == "early":
                    early[key] = value
                elif box == "scales":
                    scales = all_scales(value)

        from_end = from_middle = None
        if tick < units:
            from_end = sums_of(tick, 0, parts[part])
        elif back_tick < units:
            from_end = delta[part, back_tick]
        elif back_tick == units:
            narrow = predicted[1][parts[part]].astype(jnp.bfloat16)
            from_end = jnp.pad(narrow, ((0, 0), (0, cut - patch_width)))
        if 2 <= tick < units + 2:
            from_middle = (wide(sums_of(tick - 2, 1, parts[part])) + wide(was_middle)).astype(jnp.bfloat16)
        elif 2 <= back_tick < units + 2:
            from_middle = was_middle
        if from_end is None or from_middle is None:
            payload = from_middle if from_end is None else from_end
        else:
            payload = jnp.where(at_end, from_end, from_middle)
        if payload is not None:
            if tick < units + 2:
                pending["sent", "end"] = payload
            ends[part, tick] = swap_end(payload)
        if 1 <= tick < units + 1:
            payload = (wide(sums_of(tick - 1, 0, parts[part])) + wide(was_end)).astype(jnp.bfloat16)
            middles[part, tick] = swap_middle(payload)
        elif 1 <= back_tick < units + 1:
            middles[part, tick] = swap_middle(was_end)

        if payload is not None and tick < 99:
            pending["sent", "last"] = payload
        for work in side_work.get((tick, part), ()):
            if work == "scales":
                pending["scales", None] = local_scales()
            elif work == "own":
                left = features[0][:batch_rows, :depth]
                pending["own", (0, 0, 1)] = dot32(left, weight_own[1])
            elif work == "features":
                features.append(group_features(1))
            else:
                group = work[0]
                if tick != 1:
                    hold = was_end if tick else payload
                    features[group] = lax.optimization_barrier((features[group], hold))[0]
                pending["sums", work] = partial_sums(*work)

        group, piece = divmod(tick - line + 1, pieces)
        if 0 <= group < groups and piece == pieces - 1 and part == late:
            total = 0.0
            for unit in range(group * pieces, (group + 1) * pieces):
                arrived = [ends[other, unit + 2] for other in range(streams)]
                preact[unit], value = finished(unit, jnp.concatenate(arrived, axis=0))
                total += value
            predicted.append(mp_sum(total, jnp.bfloat16))
            errors.append((predicted[-1] - wide(goals[group])).astype(jnp.bfloat16))

        unit = back_tick + 1
        if 0 <= unit < units:
            pending["delta", (part, unit)] = new_delta(part, unit, was_end)

        unit = back_tick - line + 1
        if 0 <= unit < units and part == streams - 1:
            group, piece = divmod(unit, pieces)
            if group < groups - 1:
                pending["early", (group, piece)] = gradient_term(unit, slice(None))
            else:
                total = None
                for step in [*range(1, inner), 0]:
                    rows = slice(step * depth, (step + 1) * depth)
                    value = gradient_term(unit, rows)
                    for other in range(groups - 1):
                        value += early[other, piece][rows]
                    if step == 0:
                        outs = adam_piece(value, total, (master, moment1, moment2), outs, piece)
                    else:
                        value = turn(value.astype(jnp.bfloat16), step)
                        total = value if total is None else (wide(total) + wide(value)).astype(
                            jnp.bfloat16
                        )

    from_ends = [ends[part, 2 * units][:, :patch_width] for part in range(streams)]
    prediction = jnp.where(at_end, predicted[0], wide(jnp.concatenate(from_ends, axis=0)))
    return (prediction, *outs)


def solution(mesh):
    placed = (
        P(("dp", "mp"), None),
        P(("dp", "mp")),
        P(("dp", "mp")),
        P(("dp", "mp")),
        P(),
        P(),
        P("mp", None),
        P("dp", None),
        P("dp", "mp"),
        P("dp", "mp"),
        P("dp", "mp"),
    )
    return jax.shard_map(
        shards,
        mesh=mesh,
        in_specs=placed,
        out_specs=(P("dp", None), P("dp", "mp"), P("dp", "mp"), P("dp", "mp"), P("dp", "mp")),
        check_vma=False,
    )
```

```python
import jax
import jax.numpy as jnp
from jax import lax
from jax.experimental import pallas as pl
from jax.experimental.pallas import tpu as pltpu
from jax.sharding import PartitionSpec as P

gelu_const = 0.7978845608028654
beta_one = 0.9
beta_two = 0.95
learn_rate = 0.01
decay_rate = 0.1
adam_epsilon = 1e-08
step_count = 20

line = 4
groups = 2
pieces = 4
streams = 2


def gelu_tanh(value):
    inner = value * (gelu_const + (gelu_const * 0.044715) * (value * value))
    half = 0.5 * value
    return half + half * jnp.tanh(inner)


def gelu_slope(value):
    square = value * value
    tangent = jnp.tanh(value * (gelu_const + (gelu_const * 0.044715) * square))
    return 0.5 * (1.0 + tangent) + value * (1.0 - tangent * tangent) * (
        0.5 * gelu_const + (1.5 * gelu_const * 0.044715) * square
    )


def dot32(left, right):
    return jnp.dot(left, right, preferred_element_type=jnp.float32)


def route(patches, row_count, target_group, target_offset, block_rows):
    model_count, batch_count = lax.axis_size("mp"), lax.axis_size("dp")
    inner = batch_count // line
    devices_all = batch_count * model_count
    columns_all = inner * model_count
    slot_total, patch_width = patches.shape
    capacity = slot_total // devices_all
    lot = capacity + 1
    occupied = jnp.arange(slot_total, dtype=jnp.int32) < row_count[0]
    column = target_group % inner * model_count + target_offset // block_rows
    owner = jnp.where(occupied, column * line + target_group // inner, devices_all)
    onehot = (owner[:, None] == jnp.arange(devices_all, dtype=jnp.int32)[None, :]).astype(
        jnp.int32
    )
    placing = jnp.sum(onehot * jnp.cumsum(onehot, axis=0), axis=1) - 1
    slot = jnp.where(occupied, owner * lot + placing, devices_all * lot)
    spread = (jnp.arange(devices_all * lot, dtype=jnp.int32)[:, None] == slot[None, :]).astype(
        jnp.bfloat16
    )
    rows = dot32(spread, patches).astype(jnp.bfloat16).reshape(devices_all, lot, patch_width)
    lanes = (placing[:, None] == jnp.arange(patch_width, dtype=jnp.int32)[None, :]).astype(
        jnp.bfloat16
    )
    shifted = onehot * (target_offset % block_rows - block_rows)[:, None]
    marks = block_rows + lax.dot_general(
        shifted.astype(jnp.bfloat16),
        lanes,
        (((0,), (0,)), ((), ())),
        preferred_element_type=jnp.float32,
    )
    last = lax.broadcasted_iota(jnp.int32, rows.shape, 1) == capacity
    outgoing = jnp.where(last, marks.astype(jnp.bfloat16)[:, None, :], rows)
    outgoing = outgoing.reshape(1, columns_all, line * lot, patch_width)
    outgoing = jnp.broadcast_to(outgoing, (line,) + outgoing.shape[1:])
    arrived = lax.all_to_all(
        outgoing.reshape(devices_all, line * lot, patch_width),
        ("dp", "mp"),
        split_axis=0,
        concat_axis=0,
        tiled=True,
    )
    places = arrived.reshape(devices_all, line, lot, patch_width)[:, :, capacity, :lot]
    places = places.astype(jnp.int32)
    offsets = jnp.arange(line, dtype=jnp.int32)[None, :, None] * block_rows
    places = jnp.where(places < block_rows, places + offsets, line * block_rows)
    gather = (
        places.reshape(1, devices_all * line * lot)
        == jnp.arange(line * block_rows, dtype=jnp.int32)[:, None]
    ).astype(jnp.bfloat16)
    return dot32(gather, arrived.reshape(devices_all * line * lot, patch_width)).astype(
        jnp.bfloat16
    )


def adam_kernel(own_ref, came_ref, master_ref, moment1_ref, moment2_ref, *refs):
    master_out, moment1_out, moment2_out, copy_out = refs[-4:]
    gradient = own_ref[...] + came_ref[...].astype(jnp.float32)
    moment1_new = beta_one * moment1_ref[...] + (1.0 - beta_one) * gradient
    moment2_new = beta_two * moment2_ref[...] + (1.0 - beta_two) * gradient * gradient
    first_fix = moment1_new / (1.0 - beta_one**step_count)
    second_fix = moment2_new / (1.0 - beta_two**step_count)
    master = master_ref[...]
    master_new = master - learn_rate * (
        first_fix / (jnp.sqrt(second_fix) + adam_epsilon) + decay_rate * master
    )
    master_out[...] = master_new
    moment1_out[...] = moment1_new
    moment2_out[...] = moment2_new
    copy_out[...] = master_new.astype(jnp.bfloat16)


def adam_piece(own, came, state, outs, which):
    depth, cut = own.shape
    tile = depth // 3
    piece = pl.BlockSpec((tile, cut), lambda i: (i, 0))
    column = pl.BlockSpec((tile, cut), lambda i: (i, which))
    whole = [jax.ShapeDtypeStruct(state[0].shape, jnp.float32)] * 3
    whole.append(jax.ShapeDtypeStruct(state[0].shape, jnp.bfloat16))
    outs = outs or []
    return pl.pallas_call(
        adam_kernel,
        grid=(3,),
        in_specs=[piece, piece, column, column, column]
        + [pl.BlockSpec(memory_space=pl.ANY)] * len(outs),
        out_specs=[column] * 4,
        out_shape=whole,
        input_output_aliases={5 + i: i for i in range(len(outs))},
        compiler_params=pltpu.CompilerParams(vmem_limit_bytes=24 * 1024 * 1024),
        cost_estimate=pl.CostEstimate(
            flops=20 * depth * cut, bytes_accessed=32 * depth * cut, transcendentals=depth * cut
        ),
        name="adam_piece",
    )(own, came, *state, *outs)


def shards(
    patches,
    row_count,
    target_group,
    target_offset,
    embed,
    norm_gain,
    readout,
    target,
    master,
    moment1,
    moment2,
):
    model_count, batch_count = lax.axis_size("mp"), lax.axis_size("dp")
    inner = batch_count // line
    place = lax.axis_index("dp") // inner
    inside = lax.axis_index("dp") % inner
    last = line - 1
    at_end = (place == 0) | (place == last)
    far_side = place >= line // 2
    batch_rows = target.shape[0]
    block_rows = batch_rows // model_count
    width = embed.shape[1]
    patch_width = embed.shape[0]
    depth, columns = master.shape
    width_scale = 1.0 / width**0.5

    def swap(value, partners):
        pairs = [
            (p * inner + q, r * inner + q)
            for one, two in partners
            for p, r in ((one, two), (two, one))
            for q in range(inner)
        ]
        return lax.ppermute(value, "dp", pairs)

    def swap_end(value):
        return swap(value, ((0, 1), (last - 1, last)))

    def swap_middle(value):
        return swap(value, ((1, 2),))

    def turn(value, step):
        pairs = [
            (p * inner + q, p * inner + (q + step) % inner)
            for p in range(line)
            for q in range(inner)
        ]
        return lax.ppermute(value, "dp", pairs)

    def mp_sum(value, kind):
        step = 1
        while step < model_count:
            value = value.astype(kind)
            other = lax.ppermute(value, "mp", [(m, m ^ step) for m in range(model_count)])
            value = value.astype(jnp.float32) + other.astype(jnp.float32)
            step *= 2
        return value

    cut = columns // pieces
    lot = pieces // 2
    slices = [slice(piece * cut, (piece + 1) * cut) for piece in range(pieces)]
    weight_own = [
        master[:, first * cut : (first + lot) * cut].astype(jnp.bfloat16)
        for first in range(0, pieces, lot)
    ]
    weight_own[0], patches, target_offset = lax.optimization_barrier(
        (weight_own[0], patches, target_offset)
    )
    weight = []

    def gather_weight():
        rows = weight_own[len(weight)]
        if weight:
            rows, weight[-1] = lax.optimization_barrier((rows, weight[-1]))
        weight.append([rows] + [turn(rows, -step) for step in range(1, inner)])

    gather_weight()
    target_other = swap_end(target)

    blocks = route(patches, row_count, target_group, target_offset, block_rows)
    batches = lax.all_gather(blocks.reshape(line, block_rows, -1), "mp", axis=1, tiled=True)
    outbound = [jnp.where(far_side, batches[g], batches[last - g]) for g in range(groups)]
    inbound = [jnp.where(far_side, batches[last - g], batches[g]) for g in range(groups)]

    starts = [(place * inner + (inside + step) % inner) * depth for step in range(inner)]
    embed_here = jnp.concatenate(
        [lax.dynamic_slice_in_dim(embed, start, depth, axis=1) for start in starts], axis=1
    )
    gain_here = jnp.concatenate(
        [lax.dynamic_slice_in_dim(norm_gain, start, depth, axis=0) for start in starts], axis=0
    ).astype(jnp.float32)

    def make_features(tokens):
        return (gelu_tanh(dot32(tokens, embed_here)) * gain_here).astype(jnp.bfloat16)

    def local_scales():
        share = lax.axis_index("mp") * block_rows
        mine = jnp.concatenate(
            [lax.dynamic_slice_in_dim(tokens, share, block_rows, axis=0) for tokens in inbound],
            axis=0,
        )
        hidden = gelu_tanh(dot32(mine, embed))
        return lax.rsqrt(jnp.mean(hidden * hidden, axis=-1) + 1e-05) * width_scale

    def all_scales(scale):
        placed = jnp.zeros((groups, model_count, block_rows), jnp.float32)
        placed = lax.dynamic_update_slice_in_dim(
            placed, scale.reshape(groups, 1, block_rows), lax.axis_index("mp"), axis=1
        )
        placed = mp_sum(placed.reshape(groups, batch_rows), jnp.float32)
        return [placed[g][:, None] for g in range(groups)]

    units = groups * pieces
    goals = [target, target_other]
    rows_each = batch_rows // streams
    parts = [slice(part * rows_each, (part + 1) * rows_each) for part in range(streams)]
    features, scales, predicted, errors = [], [], [], []
    sums, preact, delta = {}, {}, {}
    ends, middles = {}, {}
    early, pending, outs = {}, {}, None

    def wide(value):
        return value.astype(jnp.float32)

    def group_features(group):
        return make_features(jnp.concatenate([outbound[group], inbound[group]], axis=0))

    joined, own_sums = {}, {}

    def partial_sums(group, side, which):
        if (group, side, which) in own_sums:
            value = own_sums[group, side, which]
            for step in range(1, inner):
                rows = slice(step * depth, (step + 1) * depth)
                left = features[group][side * batch_rows :][:batch_rows, rows]
                value += dot32(left, weight[which][step])
            return value.astype(jnp.bfloat16)
        if which not in joined:
            joined[which] = jnp.concatenate(weight[which], axis=0)
        left = features[group][side * batch_rows :][:batch_rows]
        return dot32(left, joined[which]).astype(jnp.bfloat16)

    def sums_of(unit, side, rows=slice(None)):
        group, piece = divmod(unit, pieces)
        return sums[group, side, piece // lot][rows, slices[piece % lot]]

    def finished(unit, before):
        group, piece = divmod(unit, pieces)
        value = (wide(sums_of(unit, 1)) + wide(before)) * scales[group]
        active = gelu_tanh(value).astype(jnp.bfloat16)
        return value, dot32(active, readout[slices[piece]])

    def new_delta(part, unit, before):
        group, piece = divmod(unit, pieces)
        back = lax.dot_general(
            lax.optimization_barrier((errors[group][parts[part]], before))[0],
            readout[slices[piece]],
            (((1,), (1,)), ((), ())),
            preferred_element_type=jnp.float32,
        )
        slope = gelu_slope(preact[unit][parts[part]])
        return (back * slope * scales[group][parts[part]]).astype(jnp.bfloat16)

    def gradient_term(unit, rows):
        first = units + unit
        arrived = [
            jnp.where(at_end, ends[part, first + 2], middles[part, first + 1])
            for part in range(streams)
        ] + [jnp.where(at_end, delta[part, unit], ends[part, first]) for part in range(streams)]
        return lax.dot_general(
            features[unit // pieces][:, rows],
            jnp.concatenate(arrived, axis=0),
            (((0,), (0,)), ((), ())),
            preferred_element_type=jnp.float32,
        )

    features.append(group_features(0))
    sums[0, 0, 0] = partial_sums(0, 0, 0)
    gather_weight()
    late = streams - 1
    side_work = {
        (0, 0): [(0, 1, 0), "scales", "features"],
        (0, late): [(1, 0, 0), (1, 1, 0), "own"],
        (1, late): [(0, 0, 1)],
(3, 0): [(0, 1, 1)],
        (4, 0): [(1, 0, 1)],
        (5, 0): [(1, 1, 1)],
    }
    for tick, part in [(t, p) for t in range(2 * units + line) for p in range(streams)]:
        back_tick = tick - units
        was_end = was_middle = None
        if tick:
            was_end, was_middle, pending = lax.optimization_barrier(
                (ends.get((part, tick - 1)), middles.get((part, tick - 1)), pending)
            )
            ends[part, tick - 1], middles[part, tick - 1] = was_end, was_middle
            for box, key in list(pending):
                value = pending.pop((box, key))
                if box == "sums":
                    sums[key] = value
                elif box == "delta":
                    delta[key] = value
                elif box == "own":
                    own_sums[key] = value
                elif box == "early":
                    early[key] = value
                elif box == "scales":
                    scales = all_scales(value)

        from_end = from_middle = None
        if tick < units:
            from_end = sums_of(tick, 0, parts[part])
        elif back_tick < units:
            from_end = delta[part, back_tick]
        elif back_tick == units:
            narrow = predicted[1][parts[part]].astype(jnp.bfloat16)
            from_end = jnp.pad(narrow, ((0, 0), (0, cut - patch_width)))
        if 2 <= tick < units + 2:
            from_middle = (wide(sums_of(tick - 2, 1, parts[part])) + wide(was_middle)).astype(jnp.bfloat16)
        elif 2 <= back_tick < units + 2:
            from_middle = was_middle
        if from_end is None or from_middle is None:
            payload = from_middle if from_end is None else from_end
        else:
            payload = jnp.where(at_end, from_end, from_middle)
        if payload is not None:
            if tick < units + 2:
                pending["sent", "end"] = payload
            ends[part, tick] = swap_end(payload)
        if 1 <= tick < units + 1:
            payload = (wide(sums_of(tick - 1, 0, parts[part])) + wide(was_end)).astype(jnp.bfloat16)
            middles[part, tick] = swap_middle(payload)
        elif 1 <= back_tick < units + 1:
            middles[part, tick] = swap_middle(was_end)

        if payload is not None and tick < 99:
            pending["sent", "last"] = payload
        for work in side_work.get((tick, part), ()):
            if work == "scales":
                pending["scales", None] = local_scales()
            elif work == "own":
                left = features[0][:batch_rows, :depth]
                pending["own", (0, 0, 1)] = dot32(left, weight_own[1])
            elif work == "features":
                features.append(group_features(1))
            else:
                group = work[0]
                if tick != 1:
                    hold = was_end if tick else payload
                    features[group] = lax.optimization_barrier((features[group], hold))[0]
                pending["sums", work] = partial_sums(*work)

        group, piece = divmod(tick - line + 1, pieces)
        if 0 <= group < groups and piece == pieces - 1 and part == late:
            total = 0.0
            for unit in range(group * pieces, (group + 1) * pieces):
                arrived = [ends[other, unit + 2] for other in range(streams)]
                preact[unit], value = finished(unit, jnp.concatenate(arrived, axis=0))
                total += value
            predicted.append(mp_sum(total, jnp.bfloat16))
            errors.append((predicted[-1] - wide(goals[group])).astype(jnp.bfloat16))

        unit = back_tick + 1
        if 0 <= unit < units:
            pending["delta", (part, unit)] = new_delta(part, unit, was_end)

        unit = back_tick - line + 1
        if 0 <= unit < units and part == streams - 1:
            group, piece = divmod(unit, pieces)
            if group < groups - 1:
                pending["early", (group, piece)] = gradient_term(unit, slice(None))
            else:
                total = None
                for step in [*range(1, inner), 0]:
                    rows = slice(step * depth, (step + 1) * depth)
                    value = gradient_term(unit, rows)
                    for other in range(groups - 1):
                        value += early[other, piece][rows]
                    if step == 0:
                        outs = adam_piece(value, total, (master, moment1, moment2), outs, piece)
                    else:
                        value = turn(value.astype(jnp.bfloat16), step)
                        total = value if total is None else (wide(total) + wide(value)).astype(
                            jnp.bfloat16
                        )

    from_ends = [ends[part, 2 * units][:, :patch_width] for part in range(streams)]
    prediction = jnp.where(at_end, predicted[0], wide(jnp.concatenate(from_ends, axis=0)))
    return (prediction, *outs)


def solution(mesh):
    placed = (
        P(("dp", "mp"), None),
        P(("dp", "mp")),
        P(("dp", "mp")),
        P(("dp", "mp")),
        P(),
        P(),
        P("mp", None),
        P("dp", None),
        P("dp", "mp"),
        P("dp", "mp"),
        P("dp", "mp"),
    )
    return jax.shard_map(
        shards,
        mesh=mesh,
        in_specs=placed,
        out_specs=(P("dp", None), P("dp", "mp"), P("dp", "mp"), P("dp", "mp"), P("dp", "mp")),
        check_vma=False,
    )
```

```python
import jax
import jax.numpy as jnp
from jax import lax
from jax.experimental import pallas as pl
from jax.experimental.pallas import tpu as pltpu
from jax.sharding import PartitionSpec as P

gelu_const = 0.7978845608028654
beta_one = 0.9
beta_two = 0.95
learn_rate = 0.01
decay_rate = 0.1
adam_epsilon = 1e-08
step_count = 20

line = 4
groups = 2
pieces = 4
streams = 2


def gelu_tanh(value):
    inner = value * (gelu_const + (gelu_const * 0.044715) * (value * value))
    half = 0.5 * value
    return half + half * jnp.tanh(inner)


def gelu_slope(value):
    square = value * value
    tangent = jnp.tanh(value * (gelu_const + (gelu_const * 0.044715) * square))
    return 0.5 * (1.0 + tangent) + value * (1.0 - tangent * tangent) * (
        0.5 * gelu_const + (1.5 * gelu_const * 0.044715) * square
    )


def dot32(left, right):
    return jnp.dot(left, right, preferred_element_type=jnp.float32)


def route(patches, row_count, target_group, target_offset, block_rows):
    model_count, batch_count = lax.axis_size("mp"), lax.axis_size("dp")
    inner = batch_count // line
    devices_all = batch_count * model_count
    columns_all = inner * model_count
    slot_total, patch_width = patches.shape
    capacity = slot_total // devices_all
    lot = capacity + 1
    occupied = jnp.arange(slot_total, dtype=jnp.int32) < row_count[0]
    column = target_group % inner * model_count + target_offset // block_rows
    owner = jnp.where(occupied, column * line + target_group // inner, devices_all)
    onehot = (owner[:, None] == jnp.arange(devices_all, dtype=jnp.int32)[None, :]).astype(
        jnp.int32
    )
    placing = jnp.sum(onehot * jnp.cumsum(onehot, axis=0), axis=1) - 1
    slot = jnp.where(occupied, owner * lot + placing, devices_all * lot)
    spread = (jnp.arange(devices_all * lot, dtype=jnp.int32)[:, None] == slot[None, :]).astype(
        jnp.bfloat16
    )
    rows = dot32(spread, patches).astype(jnp.bfloat16).reshape(devices_all, lot, patch_width)
    lanes = (placing[:, None] == jnp.arange(patch_width, dtype=jnp.int32)[None, :]).astype(
        jnp.bfloat16
    )
    shifted = onehot * (target_offset % block_rows - block_rows)[:, None]
    marks = block_rows + lax.dot_general(
        shifted.astype(jnp.bfloat16),
        lanes,
        (((0,), (0,)), ((), ())),
        preferred_element_type=jnp.float32,
    )
    last = lax.broadcasted_iota(jnp.int32, rows.shape, 1) == capacity
    outgoing = jnp.where(last, marks.astype(jnp.bfloat16)[:, None, :], rows)
    outgoing = outgoing.reshape(1, columns_all, line * lot, patch_width)
    outgoing = jnp.broadcast_to(outgoing, (line,) + outgoing.shape[1:])
    arrived = lax.all_to_all(
        outgoing.reshape(devices_all, line * lot, patch_width),
        ("dp", "mp"),
        split_axis=0,
        concat_axis=0,
        tiled=True,
    )
    places = arrived.reshape(devices_all, line, lot, patch_width)[:, :, capacity, :lot]
    places = places.astype(jnp.int32)
    offsets = jnp.arange(line, dtype=jnp.int32)[None, :, None] * block_rows
    places = jnp.where(places < block_rows, places + offsets, line * block_rows)
    gather = (
        places.reshape(1, devices_all * line * lot)
        == jnp.arange(line * block_rows, dtype=jnp.int32)[:, None]
    ).astype(jnp.bfloat16)
    return dot32(gather, arrived.reshape(devices_all * line * lot, patch_width)).astype(
        jnp.bfloat16
    )


def adam_kernel(own_ref, came_ref, master_ref, moment1_ref, moment2_ref, *refs):
    master_out, moment1_out, moment2_out, copy_out = refs[-4:]
    gradient = own_ref[...] + came_ref[...].astype(jnp.float32)
    moment1_new = beta_one * moment1_ref[...] + (1.0 - beta_one) * gradient
    moment2_new = beta_two * moment2_ref[...] + (1.0 - beta_two) * gradient * gradient
    first_fix = moment1_new / (1.0 - beta_one**step_count)
    second_fix = moment2_new / (1.0 - beta_two**step_count)
    master = master_ref[...]
    master_new = master - learn_rate * (
        first_fix / (jnp.sqrt(second_fix) + adam_epsilon) + decay_rate * master
    )
    master_out[...] = master_new
    moment1_out[...] = moment1_new
    moment2_out[...] = moment2_new
    copy_out[...] = master_new.astype(jnp.bfloat16)


def adam_piece(own, came, state, outs, which):
    depth, cut = own.shape
    tile = depth // 3
    piece = pl.BlockSpec((tile, cut), lambda i: (i, 0))
    column = pl.BlockSpec((tile, cut), lambda i: (i, which))
    whole = [jax.ShapeDtypeStruct(state[0].shape, jnp.float32)] * 3
    whole.append(jax.ShapeDtypeStruct(state[0].shape, jnp.bfloat16))
    outs = outs or []
    return pl.pallas_call(
        adam_kernel,
        grid=(3,),
        in_specs=[piece, piece, column, column, column]
        + [pl.BlockSpec(memory_space=pl.ANY)] * len(outs),
        out_specs=[column] * 4,
        out_shape=whole,
        input_output_aliases={5 + i: i for i in range(len(outs))},
        compiler_params=pltpu.CompilerParams(vmem_limit_bytes=24 * 1024 * 1024),
        cost_estimate=pl.CostEstimate(
            flops=20 * depth * cut, bytes_accessed=32 * depth * cut, transcendentals=depth * cut
        ),
        name="adam_piece",
    )(own, came, *state, *outs)


def shards(
    patches,
    row_count,
    target_group,
    target_offset,
    embed,
    norm_gain,
    readout,
    target,
    master,
    moment1,
    moment2,
):
    model_count, batch_count = lax.axis_size("mp"), lax.axis_size("dp")
    inner = batch_count // line
    place = lax.axis_index("dp") // inner
    inside = lax.axis_index("dp") % inner
    last = line - 1
    at_end = (place == 0) | (place == last)
    far_side = place >= line // 2
    batch_rows = target.shape[0]
    block_rows = batch_rows // model_count
    width = embed.shape[1]
    patch_width = embed.shape[0]
    depth, columns = master.shape
    width_scale = 1.0 / width**0.5

    def swap(value, partners):
        pairs = [
            (p * inner + q, r * inner + q)
            for one, two in partners
            for p, r in ((one, two), (two, one))
            for q in range(inner)
        ]
        return lax.ppermute(value, "dp", pairs)

    def swap_end(value):
        return swap(value, ((0, 1), (last - 1, last)))

    def swap_middle(value):
        return swap(value, ((1, 2),))

    def turn(value, step):
        pairs = [
            (p * inner + q, p * inner + (q + step) % inner)
            for p in range(line)
            for q in range(inner)
        ]
        return lax.ppermute(value, "dp", pairs)

    def mp_sum(value, kind):
        step = 1
        while step < model_count:
            value = value.astype(kind)
            other = lax.ppermute(value, "mp", [(m, m ^ step) for m in range(model_count)])
            value = value.astype(jnp.float32) + other.astype(jnp.float32)
            step *= 2
        return value

    cut = columns // pieces
    lot = pieces // 2
    slices = [slice(piece * cut, (piece + 1) * cut) for piece in range(pieces)]
    weight_own = [
        master[:, first * cut : (first + lot) * cut].astype(jnp.bfloat16)
        for first in range(0, pieces, lot)
    ]
    weight_own[0], patches, target_offset = lax.optimization_barrier(
        (weight_own[0], patches, target_offset)
    )
    weight = []

    def gather_weight():
        rows = weight_own[len(weight)]
        if weight:
            rows, weight[-1] = lax.optimization_barrier((rows, weight[-1]))
        weight.append([rows] + [turn(rows, -step) for step in range(1, inner)])

    gather_weight()
    target_other = swap_end(target)

    blocks = route(patches, row_count, target_group, target_offset, block_rows)
    batches = lax.all_gather(blocks.reshape(line, block_rows, -1), "mp", axis=1, tiled=True)
    outbound = [jnp.where(far_side, batches[g], batches[last - g]) for g in range(groups)]
    inbound = [jnp.where(far_side, batches[last - g], batches[g]) for g in range(groups)]

    starts = [(place * inner + (inside + step) % inner) * depth for step in range(inner)]
    embed_here = jnp.concatenate(
        [lax.dynamic_slice_in_dim(embed, start, depth, axis=1) for start in starts], axis=1
    )
    gain_here = jnp.concatenate(
        [lax.dynamic_slice_in_dim(norm_gain, start, depth, axis=0) for start in starts], axis=0
    ).astype(jnp.float32)

    def make_features(tokens):
        return (gelu_tanh(dot32(tokens, embed_here)) * gain_here).astype(jnp.bfloat16)

    def local_scales():
        share = lax.axis_index("mp") * block_rows
        mine = jnp.concatenate(
            [lax.dynamic_slice_in_dim(tokens, share, block_rows, axis=0) for tokens in inbound],
            axis=0,
        )
        hidden = gelu_tanh(dot32(mine, embed))
        return lax.rsqrt(jnp.mean(hidden * hidden, axis=-1) + 1e-05) * width_scale

    def all_scales(scale):
        placed = jnp.zeros((groups, model_count, block_rows), jnp.float32)
        placed = lax.dynamic_update_slice_in_dim(
            placed, scale.reshape(groups, 1, block_rows), lax.axis_index("mp"), axis=1
        )
        placed = mp_sum(placed.reshape(groups, batch_rows), jnp.float32)
        return [placed[g][:, None] for g in range(groups)]

    units = groups * pieces
    goals = [target, target_other]
    rows_each = batch_rows // streams
    parts = [slice(part * rows_each, (part + 1) * rows_each) for part in range(streams)]
    features, scales, predicted, errors = [], [], [], []
    sums, preact, delta = {}, {}, {}
    ends, middles = {}, {}
    early, pending, outs = {}, {}, None

    def wide(value):
        return value.astype(jnp.float32)

    def group_features(group):
        return make_features(jnp.concatenate([outbound[group], inbound[group]], axis=0))

    joined, own_sums = {}, {}

    def partial_sums(group, side, which):
        if (group, side, which) in own_sums:
            value = own_sums[group, side, which]
            for step in range(1, inner):
                rows = slice(step * depth, (step + 1) * depth)
                left = features[group][side * batch_rows :][:batch_rows, rows]
                value += dot32(left, weight[which][step])
            return value.astype(jnp.bfloat16)
        if which not in joined:
            joined[which] = jnp.concatenate(weight[which], axis=0)
        left = features[group][side * batch_rows :][:batch_rows]
        return dot32(left, joined[which]).astype(jnp.bfloat16)

    def sums_of(unit, side, rows=slice(None)):
        group, piece = divmod(unit, pieces)
        return sums[group, side, piece // lot][rows, slices[piece % lot]]

    def finished(unit, before):
        group, piece = divmod(unit, pieces)
        value = (wide(sums_of(unit, 1)) + wide(before)) * scales[group]
        active = gelu_tanh(value).astype(jnp.bfloat16)
        return value, dot32(active, readout[slices[piece]])

    def new_delta(part, unit, before):
        group, piece = divmod(unit, pieces)
        back = lax.dot_general(
            lax.optimization_barrier((errors[group][parts[part]], before))[0],
            readout[slices[piece]],
            (((1,), (1,)), ((), ())),
            preferred_element_type=jnp.float32,
        )
        slope = gelu_slope(preact[unit][parts[part]])
        return (back * slope * scales[group][parts[part]]).astype(jnp.bfloat16)

    def gradient_term(unit, rows):
        first = units + unit
        arrived = [
            jnp.where(at_end, ends[part, first + 2], middles[part, first + 1])
            for part in range(streams)
        ] + [jnp.where(at_end, delta[part, unit], ends[part, first]) for part in range(streams)]
        return lax.dot_general(
            features[unit // pieces][:, rows],
            jnp.concatenate(arrived, axis=0),
            (((0,), (0,)), ((), ())),
            preferred_element_type=jnp.float32,
        )

    features.append(group_features(0))
    sums[0, 0, 0] = partial_sums(0, 0, 0)
    gather_weight()
    late = streams - 1
    side_work = {
        (0, 0): [(0, 1, 0), "scales", "features"],
        (0, late): [(1, 0, 0), (1, 1, 0), "own"],
        (1, late): [(0, 0, 1)],
(3, 0): [(0, 1, 1)],
        (4, 0): [(1, 0, 1)],
        (5, 0): [(1, 1, 1)],
    }
    for tick, part in [(t, p) for t in range(2 * units + line) for p in range(streams)]:
        back_tick = tick - units
        was_end = was_middle = None
        if tick:
            was_end, was_middle, pending = lax.optimization_barrier(
                (ends.get((part, tick - 1)), middles.get((part, tick - 1)), pending)
            )
            ends[part, tick - 1], middles[part, tick - 1] = was_end, was_middle
            for box, key in list(pending):
                value = pending.pop((box, key))
                if box == "sums":
                    sums[key] = value
                elif box == "delta":
                    delta[key] = value
                elif box == "own":
                    own_sums[key] = value
                elif box == "early":
                    early[key] = value
                elif box == "scales":
                    scales = all_scales(value)

        from_end = from_middle = None
        if tick < units:
            from_end = sums_of(tick, 0, parts[part])
        elif back_tick < units:
            from_end = delta[part, back_tick]
        elif back_tick == units:
            narrow = predicted[1][parts[part]].astype(jnp.bfloat16)
            from_end = jnp.pad(narrow, ((0, 0), (0, cut - patch_width)))
        if 2 <= tick < units + 2:
            from_middle = (wide(sums_of(tick - 2, 1, parts[part])) + wide(was_middle)).astype(jnp.bfloat16)
        elif 2 <= back_tick < units + 2:
            from_middle = was_middle
        if from_end is None or from_middle is None:
            payload = from_middle if from_end is None else from_end
        else:
            payload = jnp.where(at_end, from_end, from_middle)
        if payload is not None:
            if tick < units + 2:
                pending["sent", "end"] = payload
            ends[part, tick] = swap_end(payload)
        if 1 <= tick < units + 1:
            payload = (wide(sums_of(tick - 1, 0, parts[part])) + wide(was_end)).astype(jnp.bfloat16)
            middles[part, tick] = swap_middle(payload)
        elif 1 <= back_tick < units + 1:
            middles[part, tick] = swap_middle(was_end)

        if payload is not None:
            pending["sent", "last"] = payload
        for work in side_work.get((tick, part), ()):
            if work == "scales":
                pending["scales", None] = local_scales()
            elif work == "own":
                left = features[0][:batch_rows, :depth]
                pending["own", (0, 0, 1)] = dot32(left, weight_own[1])
            elif work == "features":
                features.append(group_features(1))
            else:
                group = work[0]
                if tick != 1:
                    hold = was_end if tick else payload
                    features[group] = lax.optimization_barrier((features[group], hold))[0]
                pending["sums", work] = partial_sums(*work)

        group, piece = divmod(tick - line + 1, pieces)
        if 0 <= group < groups and piece == pieces - 1 and part == late:
            total = 0.0
            for unit in range(group * pieces, (group + 1) * pieces):
                arrived = [ends[other, unit + 2] for other in range(streams)]
                preact[unit], value = finished(unit, jnp.concatenate(arrived, axis=0))
                total += value
            predicted.append(mp_sum(total, jnp.bfloat16))
            errors.append((predicted[-1] - wide(goals[group])).astype(jnp.bfloat16))

        unit = back_tick + 1
        if 0 <= unit < units:
            these = [part]
            if unit == (groups - 1) * pieces:
                these = range(streams) if part == late else []
            for other in these:
                pending["delta", (other, unit)] = new_delta(other, unit, was_end)

        unit = back_tick - line + 1
        if 0 <= unit < units and part == streams - 1:
            group, piece = divmod(unit, pieces)
            if group < groups - 1:
                pending["early", (group, piece)] = gradient_term(unit, slice(None))
            else:
                total = None
                for step in [*range(1, inner), 0]:
                    rows = slice(step * depth, (step + 1) * depth)
                    value = gradient_term(unit, rows)
                    for other in range(groups - 1):
                        value += early[other, piece][rows]
                    if step == 0:
                        outs = adam_piece(value, total, (master, moment1, moment2), outs, piece)
                    else:
                        value = turn(value.astype(jnp.bfloat16), step)
                        total = value if total is None else (wide(total) + wide(value)).astype(
                            jnp.bfloat16
                        )

    from_ends = [ends[part, 2 * units][:, :patch_width] for part in range(streams)]
    prediction = jnp.where(at_end, predicted[0], wide(jnp.concatenate(from_ends, axis=0)))
    return (prediction, *outs)


def solution(mesh):
    placed = (
        P(("dp", "mp"), None),
        P(("dp", "mp")),
        P(("dp", "mp")),
        P(("dp", "mp")),
        P(),
        P(),
        P("mp", None),
        P("dp", None),
        P("dp", "mp"),
        P("dp", "mp"),
        P("dp", "mp"),
    )
    return jax.shard_map(
        shards,
        mesh=mesh,
        in_specs=placed,
        out_specs=(P("dp", None), P("dp", "mp"), P("dp", "mp"), P("dp", "mp"), P("dp", "mp")),
        check_vma=False,
    )
```
